512 devices in a mesh: af: 128 (over x, y, z_lo), row: 4 (over z_hi, core).
Axes of the slice: x: 4, y: 8, z: 8 (z_hi: 2, z_lo: 4; z = z_hi * 4 + z_lo), core: 2. Of those that a mesh axis runs over, the one named last changes fastest.
Arguments:
- traces: bfloat16 [1024, 1024, 512], P('af', 'row'), may hold values from -6 to 6
- live: int32 [1024, 1024], P('af', 'row'), may hold values 0 or 1
- selected: int32 [32], replicated, may hold values from 0 to 1023, as said below
Outputs:
- multiples: float32 [32, 4, 256, 512], P(None, 'row', 'af')
The draws below stay inside these ranges and needn't reach their ends.
Inputs may be any that keep to these rules, and one draw needn't show every extreme that they name: `selected`: 32 different shot numbers in no particular order; 0 and 1023 are always among them.
All inputs are finite; a program needn't handle non-finite values. No bound on the sum of `live` on one device may be relied on, other than what follows from the above.
Results may differ from the reference program's by a relative error of at most 0.0074.
Values may be sent and summed in bfloat16 or wider, within the bound.
A program may use at most 64 MiB of HBM per device.

```python
import math
import jax
import jax.numpy as jnp
from jax import lax

NT = 512
NF = 256
O = 32
S = 1024
N_ROW = 4


def draw_selected(key, part):
    key = jax.random.fold_in(key, 5)
    first_key, second_key = jax.random.split(key)
    middle = jax.random.permutation(first_key, S - 2)[:O - 2].astype(jnp.int32) + 1
    chosen = jnp.concatenate([jnp.array([0, S - 1], dtype=jnp.int32), middle])
    return jax.random.permutation(second_key, chosen).astype(jnp.int32)


def place_ends(values, stream_key, low, largest):
    shape = values.shape
    spot = [jax.random.randint(jax.random.fold_in(stream_key, axis), (), 0, shape[axis]) for axis in range(len(shape))]
    values = values.at[tuple(spot)].set(low)
    longest = shape.index(max(shape))
    spot[longest] = (spot[longest] + 1) % shape[longest]
    return values.at[tuple(spot)].set(largest)


def block_levels(stream_key, shape, pieces, least, top_value):
    gain, own = 1.0, jax.random.fold_in(stream_key, 6)
    for dim, parts in pieces:
        draws = jnp.exp(jax.random.uniform(jax.random.fold_in(own, dim), (parts,), jnp.float32, least / len(pieces), top_value / len(pieces)))
        gain = gain * jnp.repeat(draws, shape[dim] // parts).reshape([-1 if axis == dim else 1 for axis in range(len(shape))])
    return gain


def scatter_about(key, shape, width, bound, pieces=(), kind=jnp.bfloat16):
    entries = jax.random.normal(key, shape, jnp.float32) * width
    if len(pieces) > 0:
        entries = block_levels(key, shape, pieces, -0.22, 0.18) * entries
    return jnp.clip(entries, min=-bound, max=bound).astype(kind)


def setup_inputs(seed: int = 0) -> dict:
    arg_keys = jax.random.split(jax.random.key(seed), 4)
    return {
        "traces": scatter_about(arg_keys[0], (S, S, NT), 1.0, 6.0, ((0, 128), (1, 4))),
        "live": place_ends((jax.random.randint(arg_keys[1], (S, S), 0, 4) < 3).astype(jnp.int32), jax.random.fold_in(arg_keys[1], 1), 0, 1),
        "selected": draw_selected(jax.random.fold_in(arg_keys[3], 71), 0),
    }


def tables(samples, freqs):
    times_idx = jnp.arange(samples, dtype=jnp.int32)
    freq_idx = jnp.arange(freqs, dtype=jnp.int32)
    phases = (times_idx[:, None] * freq_idx[None, :] % samples).astype(jnp.float32) * (2.0 * math.pi / samples)
    norm_factor = 1.0 / math.sqrt(samples)
    forward = (jnp.concatenate([jnp.cos(phases), -jnp.sin(phases)], axis=1) * norm_factor).astype(jnp.bfloat16)
    weights = jnp.where(freq_idx == 0, 1.0, 2.0).astype(jnp.float32)
    inverse = jnp.concatenate([jnp.cos(phases) * weights[None, :], -jnp.sin(phases) * weights[None, :]], axis=1)
    inverse = (inverse.T * norm_factor).astype(jnp.bfloat16)
    return (forward, inverse)

def reference(traces, live, selected):
    forward, inverse = tables(NT, NF)
    masked = (traces * live[:, :, None].astype(jnp.bfloat16)).reshape(S * S, NT)
    nblocks = 16
    table_rows = forward.T.reshape(nblocks, 2 * NF // nblocks, NT)

    def dft_block(rows_t):
        return jnp.dot(masked, rows_t.T, preferred_element_type=jnp.float32).astype(jnp.bfloat16).T
    spectra = lax.map(dft_block, table_rows).reshape(2 * NF, S, S)
    factor = 1.0 / math.sqrt(S)

    def convolve(freq_at):
        all_real = spectra[freq_at]
        all_imag = spectra[NF + freq_at]
        sel_real = jnp.take(all_real, selected, axis=0)
        sel_imag = jnp.take(all_imag, selected, axis=0)
        part_real = (jnp.dot(sel_real, all_real, preferred_element_type=jnp.float32) - jnp.dot(sel_imag, all_imag, preferred_element_type=jnp.float32)) * factor
        part_imag = (jnp.dot(sel_real, all_imag, preferred_element_type=jnp.float32) + jnp.dot(sel_imag, all_real, preferred_element_type=jnp.float32)) * factor
        return (part_real.astype(jnp.bfloat16), part_imag.astype(jnp.bfloat16))
    reals, imags = lax.map(convolve, jnp.arange(NF, dtype=jnp.int32))
    stacked = jnp.concatenate([reals, imags], axis=0).reshape(2 * NF, O * S)
    result = jnp.dot(stacked.T, inverse, preferred_element_type=jnp.float32)
    return result.reshape(O, N_ROW, S // N_ROW, NT)
```

```python
import functools
import math

import jax
import jax.numpy as jnp
import numpy as np
from jax import lax
from jax.experimental import pallas as pl
from jax.experimental.pallas import tpu as pltpu
from jax.sharding import PartitionSpec as P

MESH = pl.DeviceIdType.MESH
BF, F32, I32 = jnp.bfloat16, jnp.float32, jnp.int32

NX, NY, NZ, NROW = 4, 8, 4, 4
NT, NF, SHOTS, RECV, OUT = 512, 256, 8, 256, 32
BANDS, PER = 32, 8
COMP = 2 * PER


def host_tables():
    t = np.arange(NT)[:, None]
    f = np.arange(NF)[None, :]
    ang = (t * f % NT) * (2.0 * math.pi / NT)
    norm = 1.0 / math.sqrt(NT)
    w = np.where(np.arange(NF) == 0, 1.0, 2.0)[:, None]
    cos, sin = np.cos(ang).T, -np.sin(ang).T
    fwd = np.stack([cos.reshape(BANDS, PER, NT), sin.reshape(BANDS, PER, NT)], axis=1) * norm
    inv = np.concatenate([cos * w, sin * w], axis=0) * norm
    as_bf = lambda a: a.astype(np.float32).astype(jnp.bfloat16)
    return as_bf(fwd.reshape(2 * NF, NT)), as_bf(inv)


def af(x, y, z):
    return (x * NY + y) * NZ + z


def base_of(y):
    return (y - 2 + y % 2 + NY) % NY


def iota(shape, dim):
    return lax.broadcasted_iota(I32, shape, dim)


def mm(a, b, dims=((1,), (0,))):
    return lax.dot_general(a, b, (dims, ((), ())), preferred_element_type=F32)


def kernel(
    sel_ref, traces_hbm, live_ref, fwd_hbm, inv_hbm, out_ref,
    traces, fwd, inv, send, recv, bt, perm, pick, lanes, spread,
    a_own, a_msg, a_in, a_row, p2, stage, r_send, r_recv,
    load_sem, send_sem, recv_sem, own_sem, a_send_sem, a_recv_sem, row_send_sem, row_recv_sem,
    r_send_sem, r_recv_sem, r_own_sem,
):
    a = lax.axis_index("af")
    row = lax.axis_index("row")
    x, y, z = a // (NY * NZ), (a // NZ) % NY, a % NZ
    half = y // 2
    zp, zs = z // 2, z % 2
    base = base_of(y)
    cores = (a, row // 2 * 2 + 1 - row % 2)
    across = (a, (row + 2) % NROW)

    def home(u):
        return af(x, (y + 4 * (u // 2)) % NY, (z + 2 * (u % 2)) % NZ)

    fwd_copy = pltpu.make_async_copy(fwd_hbm, fwd, load_sem.at[SHOTS])
    inv_copy = pltpu.make_async_copy(inv_hbm, inv, load_sem.at[SHOTS + 1])
    fwd_copy.start()
    loads = [pltpu.make_async_copy(traces_hbm.at[s], traces.at[s], load_sem.at[s]) for s in range(SHOTS)]
    for c in loads:
        c.start()
    inv_copy.start()

    barrier = pltpu.get_barrier_semaphore()

    @pl.loop(1, BANDS)
    def _(i):
        sx = (x + i // 8) % NX
        sy = (base + ((y - base + NY) % NY + (i // 2) % 4) % 4) % NY
        sz = 2 * zp + (zs + i) % 2
        pl.semaphore_signal(barrier, inc=1, device_id=(af(sx, sy, sz), row), device_id_type=MESH)

    @pl.loop(1, 4)
    def _(u):
        pl.semaphore_signal(barrier, inc=1, device_id=(home(u), row), device_id_type=MESH)

    pl.semaphore_signal(barrier, inc=1, device_id=cores, device_id_type=MESH)
    pl.semaphore_signal(barrier, inc=1, device_id=across, device_id_type=MESH)

    fwd_copy.wait()
    for c in loads:
        c.wait()
    live = live_ref[...].astype(F32)

    def band_copy(dx, w, dz):
        bx = (x + dx) % NX
        hy = (2 * half - 1 + (y % 2 + 1 + w) % 4 + NY) % NY
        bz = (zs + dz) % 2
        band = bx * 8 + (hy % 4) * 2 + bz
        slot = x * 8 + ((y - base_of(hy) + NY) % NY) * 2 + zs
        return pltpu.make_async_remote_copy(
            src_ref=send.at[band], dst_ref=recv.at[slot], send_sem=send_sem,
            recv_sem=recv_sem.at[slot], device_id=(af(bx, hy, 2 * zp + bz), row), device_id_type=MESH,
        )

    own_band = x * 8 + (y % 4) * 2 + zs
    own_slot = x * 8 + ((y - base + NY) % NY) * 2 + zs
    own_copy = pltpu.make_async_copy(send.at[own_band], recv.at[own_slot], own_sem)

    @pl.loop(0, NX)
    def _(i):
        dx = (i + 1) % NX
        bx = (x + dx) % NX
        table = fwd[pl.ds(pl.multiple_of(bx * 128, 128), 128), :]
        for s in range(SHOTS):
            spec = mm(table, traces[s], ((1,), (1,))) * live[s : s + 1, :]
            send[pl.ds(bx * 8, 8), s] = spec.astype(BF).reshape(8, COMP, RECV)

        @pl.when(i == 0)
        def _():
            pl.semaphore_wait(barrier, BANDS - 1 + 3 + 2)

        @pl.loop(0, 8)
        def _(j):
            w, dz = j // 2, j % 2

            @pl.when(dx + j != 0)
            def _():
                band_copy(dx, w, dz).start()

    own_copy.start()

    ro, co = iota((256, 256), 0), iota((256, 256), 1)
    perm[...] = jnp.where(co == (ro % 16) // 8 * 128 + ro % 8 * 16 + ro // 16, 1.0, 0.0).astype(BF)
    j = iota((1, 512), 1)
    k64 = j % 64
    shot = ((j // 128 * NY + (base + k64 // 16) % NY) * NZ + 2 * zp + k64 // 8 % 2) * SHOTS + k64 % 8
    part = j % 128 // 64
    o_at = iota((OUT, 512), 0)
    want = jnp.full((OUT, 512), -1, I32)
    for o in range(OUT):
        want = jnp.where(o_at == o, sel_ref[o], want)
    hit = want == shot
    pick[0:OUT, :] = jnp.where(hit & (part == 0), 1.0, 0.0).astype(BF)
    pick[OUT : 2 * OUT, :] = jnp.where(hit & (part == 1), 1.0, 0.0).astype(BF)
    u = j // 128
    k_here = ((base + 4 * (u // 2) + k64 // 16) % NY * NZ + 2 * ((zp + u) % 2) + k64 // 8 % 2) * 8 + k64 % 8
    from_row = part * RECV + k_here
    lanes[...] = jnp.where(iota((512, 512), 0) == from_row, 1.0, 0.0).astype(BF)
    d_at = iota((128, 512), 0)
    j2 = iota((128, 512), 1)
    spread[...] = jnp.where(j2 % 256 == 2 * d_at + j2 // 256, 1.0, 0.0).astype(BF)
    p2[...] = jnp.zeros_like(p2)

    own_copy.wait()

    @pl.loop(0, NX)
    def _(i):
        sx = (x + 2 * NX - 1 - i) % NX

        @pl.loop(0, 4)
        def _(ys):
            for b in range(2):
                slot = sx * 8 + ys * 2 + b

                @pl.when(slot != own_slot)
                def _():
                    pltpu.make_async_remote_copy(
                        src_ref=send.at[0], dst_ref=recv.at[slot], send_sem=send_sem,
                        recv_sem=recv_sem.at[slot], device_id=cores, device_id_type=MESH,
                    ).wait_recv()

            block = recv[pl.ds(sx * 8 + ys * 2, 2)].reshape(256, RECV)
            turned = mm(perm[...], block).astype(BF).reshape(2, PER, 16, RECV)
            bt[:, sx, 0, ys] = turned[0]
            bt[:, sx, 1, ys] = turned[1]

    for f in range(PER):
        got = mm(pick[...], bt[f].reshape(512, RECV)).astype(BF)
        a_own[f * OUT : (f + 1) * OUT, 0:RECV] = got[0:OUT]
        a_own[f * OUT : (f + 1) * OUT, RECV:] = got[OUT:]
    for v in range(4):
        a_msg[v] = mm(a_own[...], lanes[:, v * 128 : (v + 1) * 128]).astype(BF)

    def home_copy(v):
        return pltpu.make_async_remote_copy(
            src_ref=a_msg.at[v], dst_ref=a_in.at[v], send_sem=a_send_sem.at[v],
            recv_sem=a_recv_sem.at[v], device_id=(home(v), row), device_id_type=MESH,
        )

    for v in (3, 2, 1):
        home_copy(v).start()
    for v in (1, 2, 3):
        home_copy(v).wait()
    a_row[row] = a_msg[0] + a_in[1] + a_in[2] + a_in[3]

    other = (row + 2) % NROW

    def row_copy(slot, to, sem):
        return pltpu.make_async_remote_copy(
            src_ref=a_row.at[slot], dst_ref=a_row.at[slot], send_sem=row_send_sem.at[sem],
            recv_sem=row_recv_sem.at[sem], device_id=to, device_id_type=MESH,
        )

    first, second, third = row_copy(row, across, 0), row_copy(row, cores, 1), row_copy(other, cores, 2)
    first.start()
    second.start()
    first.wait_recv()
    third.start()
    second.wait_recv()
    third.wait_recv()

    sign = jnp.where(iota((1, 128), 1) < 64, 1.0, -1.0)
    left = []
    for v in range(NROW):
        val = a_row[v].astype(F32)
        left.append(((val * sign).astype(BF), pltpu.roll(val, 64, 1).astype(BF)))
    factor = 1.0 / math.sqrt(NX * NY * NZ * SHOTS)
    for f in range(PER):
        rows = slice(f * OUT, (f + 1) * OUT)
        lhs = jnp.concatenate(
            [jnp.concatenate([left[v][part_][rows] for v in range(NROW)], axis=1) for part_ in range(2)], axis=0
        )
        pred = (mm(lhs, bt[f].reshape(512, RECV)) * factor).astype(BF)
        p2[f, 0:64, 0:RECV] = pred
        p2[f, 64:128, RECV:] = pred

    for f in range(PER):
        stage[pl.ds(f, 128, stride=8), :] = mm(spread[...], p2[f], ((1,), (1,)))
    r_send[...] = stage[...].astype(BF).reshape(128, 8, 128)

    my_slot = (y // 4 * 2 + zp) * BANDS + own_band
    own_r = pltpu.make_async_copy(r_send.at[a], r_recv.at[my_slot], r_own_sem)
    own_r.start()

    @pl.loop(1, 128)
    def _(i):
        d = (a + i * 47) % 128
        pltpu.make_async_remote_copy(
            src_ref=r_send.at[d], dst_ref=r_recv.at[my_slot], send_sem=r_send_sem,
            recv_sem=r_recv_sem, device_id=(d, row), device_id_type=MESH,
        ).start()

    all_r = pltpu.make_async_remote_copy(
        src_ref=r_send.at[pl.ds(0, 127)], dst_ref=r_recv.at[pl.ds(0, 127)], send_sem=r_send_sem,
        recv_sem=r_recv_sem, device_id=cores, device_id_type=MESH,
    )
    inv_copy.wait()
    own_r.wait()
    all_r.wait_recv()

    total = r_recv[0:32].astype(F32)
    for v in range(1, 4):
        total = total + r_recv[v * 32 : (v + 1) * 32].astype(F32)
    turned = total.reshape(256, 128).T.astype(BF)
    lhs = jnp.concatenate(
        [jnp.concatenate([turned[r * 64 : r * 64 + 32], turned[r * 64 + 32 : r * 64 + 64]], axis=1) for r in range(2)],
        axis=0,
    )
    res = mm(lhs, inv[...])
    for r in range(2):
        out_ref[r] = res[r * 32 : (r + 1) * 32]

    all_r.wait_send()
    for c in (first, second, third):
        c.wait_send()
    pltpu.make_async_remote_copy(
        src_ref=send.at[pl.ds(0, 31)], dst_ref=recv.at[pl.ds(0, 31)], send_sem=send_sem,
        recv_sem=recv_sem.at[0], device_id=cores, device_id_type=MESH,
    ).wait_send()


def per_device(traces, live, selected):
    fwd, inv = host_tables()
    any_, vmem = pl.BlockSpec(memory_space=pl.ANY), pl.BlockSpec(memory_space=pltpu.VMEM)
    dma = pltpu.SemaphoreType.DMA
    out = pl.pallas_call(
        kernel,
        out_shape=jax.ShapeDtypeStruct((2, OUT, NT), F32),
        in_specs=[pl.BlockSpec(memory_space=pltpu.SMEM), any_, vmem, any_, any_],
        out_specs=vmem,
        scratch_shapes=[
            pltpu.VMEM((SHOTS, RECV, NT), BF),
            pltpu.VMEM((2 * NF, NT), BF),
            pltpu.VMEM((2 * NF, NT), BF),
            pltpu.VMEM((BANDS, SHOTS, COMP, RECV), BF),
            pltpu.VMEM((BANDS, SHOTS, COMP, RECV), BF),
            pltpu.VMEM((PER, NX, 2, 4, 16, RECV), BF),
            pltpu.VMEM((256, 256), BF),
            pltpu.VMEM((2 * OUT, 512), BF),
            pltpu.VMEM((512, 512), BF),
            pltpu.VMEM((128, 512), BF),
            pltpu.VMEM((PER * OUT, 512), BF),
            pltpu.VMEM((4, PER * OUT, 128), BF),
            pltpu.VMEM((4, PER * OUT, 128), BF),
            pltpu.VMEM((NROW, PER * OUT, 128), BF),
            pltpu.VMEM((PER, 128, 512), BF),
            pltpu.VMEM((1024, 128), F32),
            pltpu.VMEM((128, 8, 128), BF),
            pltpu.VMEM((128, 8, 128), BF),
            dma((SHOTS + 2,)), dma, dma((BANDS,)), dma, dma((4,)), dma((4,)), dma((3,)), dma((3,)),
            dma, dma, dma,
        ],
        compiler_params=pltpu.CompilerParams(
            collective_id=0, has_side_effects=True, vmem_limit_bytes=40 << 20
        ),
        cost_estimate=pl.CostEstimate(flops=2 << 30, bytes_accessed=4 << 20, transcendentals=0),
        name="multiples",
    )(selected, traces, live, jnp.asarray(fwd), jnp.asarray(inv))
    return out.transpose(1, 0, 2)[:, None]


def solution(mesh):
    in_specs = (P("af", "row", None), P("af", "row"), P())
    out_specs = P(None, "row", "af", None)
    return jax.shard_map(per_device, mesh=mesh, in_specs=in_specs, out_specs=out_specs, check_vma=False)
```

```python
import functools
import math

import jax
import jax.numpy as jnp
import numpy as np
from jax import lax
from jax.experimental import pallas as pl
from jax.experimental.pallas import tpu as pltpu
from jax.sharding import PartitionSpec as P

MESH = pl.DeviceIdType.MESH
BF, F32, I32 = jnp.bfloat16, jnp.float32, jnp.int32

NX, NY, NZ, NROW = 4, 8, 4, 4
NT, NF, SHOTS, RECV, OUT = 512, 256, 8, 256, 32
BANDS, PER = 32, 8
COMP = 2 * PER
GROUPS = 2
PER_G = PER // GROUPS


def host_tables():
    t = np.arange(NT)[:, None]
    f = np.arange(NF)[None, :]
    ang = (t * f % NT) * (2.0 * math.pi / NT)
    norm = 1.0 / math.sqrt(NT)
    w = np.where(np.arange(NF) == 0, 1.0, 2.0)[:, None]
    cos, sin = np.cos(ang).T, -np.sin(ang).T
    fwd = np.stack([cos.reshape(BANDS, PER, NT), sin.reshape(BANDS, PER, NT)], axis=1) * norm
    inv = np.concatenate([cos * w, sin * w], axis=0) * norm
    as_bf = lambda a: a.astype(np.float32).astype(jnp.bfloat16)
    fwd = fwd.reshape(2 * NF, NT)
    return as_bf(np.concatenate([fwd, fwd[:128]])), as_bf(inv)


def af(x, y, z):
    return (x * NY + y) * NZ + z


def base_of(y):
    return lax.rem(y - 2 + lax.rem(y, 2) + NY, NY)


def iota(shape, dim):
    return lax.broadcasted_iota(I32, shape, dim)


def mm(a, b, dims=((1,), (0,))):
    return lax.dot_general(a, b, (dims, ((), ())), preferred_element_type=F32)


def kernel(
    sel_hbm, traces_hbm, live_hbm, fwd_hbm, inv_hbm, out_ref,
    sel_ref, live_ref, traces, fwd, inv, send, recv, bt, perm, pick, lanes, spread,
    a_own, a_msg, a_in, a_row, p2, stage, r_send, r_recv,
    load_sem, send_sem, recv_sem, own_sem, a_send_sem, a_recv_sem, row_send_sem, row_recv_sem,
    r_send_sem, r_recv_sem, r_own_sem,
):
    a = lax.axis_index("af")
    row = lax.axis_index("row")
    x, y, z = lax.div(a, NY * NZ), lax.rem(lax.div(a, NZ), NY), lax.rem(a, NZ)
    half, zp, zs, odd = lax.div(y, 2), lax.div(z, 2), lax.rem(z, 2), lax.rem(y, 2)
    base = base_of(y)
    xs = [lax.rem(x + i, NX) for i in range(NX)]
    ys = [lax.rem(y + i, NY) for i in range(NY)]
    zz = [lax.rem(z + i, NZ) for i in range(NZ)]
    other = lax.rem(row + 2, NROW)
    cores = (a, row + 1 - 2 * lax.rem(row, 2))
    across = (a, other)
    pair = [z, z + 1 - 2 * zs]
    to_y = [lax.rem(2 * half - 1 + lax.rem(odd + 1 + w, 4) + NY, NY) for w in range(4)]
    from_y = [lax.rem(base + lax.rem(lax.rem(y - base + NY, NY) + w, 4), NY) for w in range(4)]
    homes = [af(x, ys[4 * (u // 2)], zz[2 * (u % 2)]) for u in range(4)]

    fwd_copy = pltpu.make_async_copy(fwd_hbm, fwd, load_sem.at[SHOTS])
    inv_copy = pltpu.make_async_copy(inv_hbm, inv, load_sem.at[SHOTS + 1])
    live_copy = pltpu.make_async_copy(live_hbm, live_ref, load_sem.at[SHOTS + 2])
    sel_copy = pltpu.make_async_copy(sel_hbm, sel_ref, load_sem.at[SHOTS + 3])
    fwd_copy.start()
    live_copy.start()
    loads = [pltpu.make_async_copy(traces_hbm.at[s], traces.at[s], load_sem.at[s]) for s in range(SHOTS)]
    for c in loads:
        c.start()
    inv_copy.start()
    sel_copy.start()

    barrier = pltpu.get_barrier_semaphore()

    for i in range(1, BANDS):
        pl.semaphore_signal(
            barrier, inc=1, device_id=(af(xs[i // 8], from_y[i // 2 % 4], pair[i % 2]), row), device_id_type=MESH
        )
    for u in range(1, 4):
        pl.semaphore_signal(barrier, inc=1, device_id=(homes[u], row), device_id_type=MESH)
    pl.semaphore_signal(barrier, inc=1, device_id=cores, device_id_type=MESH)
    pl.semaphore_signal(barrier, inc=1, device_id=across, device_id_type=MESH)

    fwd_copy.wait()
    live_copy.wait()
    for c in loads:
        c.wait()
    live = live_ref[...].astype(F32)

    def band_of(bx, hy, hz):
        return bx * 8 + lax.rem(hy, 4) * 2 + lax.rem(hz, 2)

    to_slot = [x * 8 + lax.rem(y - base_of(hy) + NY, NY) * 2 + zs for hy in to_y]

    def band_copy(dx, w, dz):
        band, slot = band_of(xs[dx], to_y[w], pair[dz]), to_slot[w]
        return pltpu.make_async_remote_copy(
            src_ref=send.at[band], dst_ref=recv.at[slot], send_sem=send_sem,
            recv_sem=recv_sem.at[slot], device_id=(af(xs[dx], to_y[w], pair[dz]), row), device_id_type=MESH,
        )

    own_band, own_slot = band_of(x, y, z), to_slot[0]
    own_copy = pltpu.make_async_copy(send.at[own_band], recv.at[own_slot], own_sem)

    for i in range(2):
        first = xs[(1 + 2 * i) % NX]
        second = xs[(2 + 2 * i) % NX]
        table = fwd[pl.ds(pl.multiple_of(first * 128, 128), 256), :]
        for s in range(SHOTS):
            spec = (mm(table, traces[s], ((1,), (1,))) * live[s : s + 1, :]).astype(BF)
            spec = spec.reshape(2, 8, COMP, RECV)
            send[pl.ds(first * 8, 8), s] = spec[0]
            send[pl.ds(second * 8, 8), s] = spec[1]
        if i == 0:
            pl.semaphore_wait(barrier, BANDS - 1 + 3 + 2)
        for j in range(16):
            dx, w, dz = (1 + 2 * i + j % 2) % NX, (j // 2 + 1) % 4, (j // 8 + 1) % 2
            if (dx, w, dz) != (0, 0, 0):
                band_copy(dx, w, dz).start()

    own_copy.start()

    ro, co = iota((256, 256), 0), iota((256, 256), 1)
    perm[...] = jnp.where(co == (ro % 16) // 8 * 128 + ro % 8 * 16 + ro // 16, 1.0, 0.0).astype(BF)
    j = iota((1, 512), 1)
    k64 = j % 64
    shot = ((j // 128 * NY + (base + k64 // 16) % NY) * NZ + 2 * zp + k64 // 8 % 2) * SHOTS + k64 % 8
    part = j % 128 // 64
    sel_copy.wait()
    o_at = iota((OUT, 512), 0)
    want = jnp.full((OUT, 512), -1, I32)
    for o in range(OUT):
        want = jnp.where(o_at == o, sel_ref[o], want)
    hit = want == shot
    pick[0:OUT, :] = jnp.where(hit & (part == 0), 1.0, 0.0).astype(BF)
    pick[OUT : 2 * OUT, :] = jnp.where(hit & (part == 1), 1.0, 0.0).astype(BF)
    u = j // 128
    k_here = ((base + 4 * (u // 2) + k64 // 16) % NY * NZ + 2 * ((zp + u) % 2) + k64 // 8 % 2) * 8 + k64 % 8
    from_row = part * RECV + k_here
    lanes[...] = jnp.where(iota((512, 512), 0) == from_row, 1.0, 0.0).astype(BF)
    d_at = iota((128, 512), 0)
    j2 = iota((128, 512), 1)
    spread[...] = jnp.where(j2 % 256 == 2 * d_at + j2 // 256, 1.0, 0.0).astype(BF)
    p2[...] = jnp.zeros_like(p2)

    own_copy.wait()

    @pl.loop(0, NX)
    def _(i):
        sx = lax.rem(x + 2 * NX - 1 - i, NX)
        for q in range(8):
            slot = sx * 8 + q

            @pl.when(slot != own_slot)
            def _():
                pltpu.make_async_remote_copy(
                    src_ref=send.at[0], dst_ref=recv.at[slot], send_sem=send_sem,
                    recv_sem=recv_sem.at[slot], device_id=cores, device_id_type=MESH,
                ).wait_recv()

        for q in range(4):
            block = recv[pl.ds(sx * 8 + q * 2, 2)].reshape(256, RECV)
            turned = mm(perm[...], block).astype(BF).reshape(2, PER, 16, RECV)
            bt[:, sx, 0, q] = turned[0]
            bt[:, sx, 1, q] = turned[1]

    def home_copy(g, v):
        return pltpu.make_async_remote_copy(
            src_ref=a_msg.at[g, v], dst_ref=a_in.at[g, v], send_sem=a_send_sem.at[g, v],
            recv_sem=a_recv_sem.at[g, v], device_id=(homes[v], row), device_id_type=MESH,
        )

    def row_copy(g, slot, to, sem):
        return pltpu.make_async_remote_copy(
            src_ref=a_row.at[slot, g], dst_ref=a_row.at[slot, g], send_sem=row_send_sem.at[g, sem],
            recv_sem=row_recv_sem.at[g, sem], device_id=to, device_id_type=MESH,
        )

    for g in range(GROUPS):
        for f in range(PER_G):
            got = mm(pick[...], bt[g * PER_G + f].reshape(512, RECV)).astype(BF)
            a_own[g, f * OUT : (f + 1) * OUT, 0:RECV] = got[0:OUT]
            a_own[g, f * OUT : (f + 1) * OUT, RECV:] = got[OUT:]
        for v in (3, 2, 1, 0):
            a_msg[g, v] = mm(a_own[g], lanes[:, v * 128 : (v + 1) * 128]).astype(BF)
            if v:
                home_copy(g, v).start()

    to_across = [row_copy(g, row, across, 0) for g in range(GROUPS)]
    to_core = [row_copy(g, row, cores, 1) for g in range(GROUPS)]
    onward = [row_copy(g, other, cores, 2) for g in range(GROUPS)]
    for g in range(GROUPS):
        for v in (1, 2, 3):
            home_copy(g, v).wait()
        a_row[row, g] = a_msg[g, 0] + a_in[g, 1] + a_in[g, 2] + a_in[g, 3]
        to_across[g].start()
        to_core[g].start()
    for g in range(GROUPS):
        to_across[g].wait_recv()
        onward[g].start()

    sign = jnp.where(iota((1, 128), 1) < 64, 1.0, -1.0)
    factor = 1.0 / math.sqrt(NX * NY * NZ * SHOTS)
    for g in range(GROUPS):
        to_core[g].wait_recv()
        onward[g].wait_recv()
        left = []
        for v in range(NROW):
            val = a_row[v, g].astype(F32)
            left.append(((val * sign).astype(BF), pltpu.roll(val, 64, 1).astype(BF)))
        for f in range(PER_G):
            rows = slice(f * OUT, (f + 1) * OUT)
            lhs = jnp.concatenate(
                [jnp.concatenate([left[v][p][rows] for v in range(NROW)], axis=1) for p in range(2)], axis=0
            )
            at = g * PER_G + f
            pred = (mm(lhs, bt[at].reshape(512, RECV)) * factor).astype(BF)
            p2[at, 0:64, 0:RECV] = pred
            p2[at, 64:128, RECV:] = pred

    for f in range(PER):
        stage[pl.ds(f, 128, stride=8), :] = mm(spread[...], p2[f], ((1,), (1,)))
    r_send[...] = stage[...].astype(BF).reshape(128, 8, 128)

    my_slot = (lax.div(y, 4) * 2 + zp) * BANDS + own_band
    own_r = pltpu.make_async_copy(r_send.at[a], r_recv.at[my_slot], r_own_sem)
    own_r.start()

    def back(d):
        pltpu.make_async_remote_copy(
            src_ref=r_send.at[d], dst_ref=r_recv.at[my_slot], send_sem=r_send_sem,
            recv_sem=r_recv_sem, device_id=(d, row), device_id_type=MESH,
        ).start()

    @pl.loop(0, NY)
    def _(i):
        dy = lax.rem(y + 4 + i, NY)
        for j in range(1, 16):
            back(af(xs[j % NX], dy, zz[j // NX]))

        @pl.when(i != 4)
        def _():
            back(af(x, dy, z))

    all_r = pltpu.make_async_remote_copy(
        src_ref=r_send.at[pl.ds(0, 127)], dst_ref=r_recv.at[pl.ds(0, 127)], send_sem=r_send_sem,
        recv_sem=r_recv_sem, device_id=cores, device_id_type=MESH,
    )
    inv_copy.wait()
    own_r.wait()
    all_r.wait_recv()

    total = r_recv[0:32].astype(F32)
    for v in range(1, 4):
        total = total + r_recv[v * 32 : (v + 1) * 32].astype(F32)
    turned = total.reshape(256, 128).T.astype(BF)
    lhs = jnp.concatenate(
        [jnp.concatenate([turned[r * 64 : r * 64 + 32], turned[r * 64 + 32 : r * 64 + 64]], axis=1) for r in range(2)],
        axis=0,
    )
    res = mm(lhs, inv[...])
    for r in range(2):
        out_ref[r] = res[r * 32 : (r + 1) * 32]

    all_r.wait_send()
    for g in range(GROUPS):
        for c in (to_across[g], to_core[g], onward[g]):
            c.wait_send()
    pltpu.make_async_remote_copy(
        src_ref=send.at[pl.ds(0, 31)], dst_ref=recv.at[pl.ds(0, 31)], send_sem=send_sem,
        recv_sem=recv_sem.at[0], device_id=cores, device_id_type=MESH,
    ).wait_send()


def per_device(traces, live, selected):
    fwd, inv = host_tables()
    any_, vmem = pl.BlockSpec(memory_space=pl.ANY), pl.BlockSpec(memory_space=pltpu.VMEM)
    dma = pltpu.SemaphoreType.DMA
    out = pl.pallas_call(
        kernel,
        out_shape=jax.ShapeDtypeStruct((2, OUT, NT), F32),
        in_specs=[any_] * 5,
        out_specs=vmem,
        scratch_shapes=[
            pltpu.SMEM((OUT,), I32),
            pltpu.VMEM((SHOTS, RECV), I32),
            pltpu.VMEM((SHOTS, RECV, NT), BF),
            pltpu.VMEM((2 * NF + 128, NT), BF),
            pltpu.VMEM((2 * NF, NT), BF),
            pltpu.VMEM((BANDS, SHOTS, COMP, RECV), BF),
            pltpu.VMEM((BANDS, SHOTS, COMP, RECV), BF),
            pltpu.VMEM((PER, NX, 2, 4, 16, RECV), BF),
            pltpu.VMEM((256, 256), BF),
            pltpu.VMEM((2 * OUT, 512), BF),
            pltpu.VMEM((512, 512), BF),
            pltpu.VMEM((128, 512), BF),
            pltpu.VMEM((GROUPS, PER_G * OUT, 512), BF),
            pltpu.VMEM((GROUPS, 4, PER_G * OUT, 128), BF),
            pltpu.VMEM((GROUPS, 4, PER_G * OUT, 128), BF),
            pltpu.VMEM((NROW, GROUPS, PER_G * OUT, 128), BF),
            pltpu.VMEM((PER, 128, 512), BF),
            pltpu.VMEM((1024, 128), F32),
            pltpu.VMEM((128, 8, 128), BF),
            pltpu.VMEM((128, 8, 128), BF),
            dma((SHOTS + 4,)), dma, dma((BANDS,)), dma,
            dma((GROUPS, 4)), dma((GROUPS, 4)), dma((GROUPS, 3)), dma((GROUPS, 3)),
            dma, dma, dma,
        ],
        compiler_params=pltpu.CompilerParams(
            collective_id=0, has_side_effects=True, vmem_limit_bytes=60 << 20
        ),
        cost_estimate=pl.CostEstimate(flops=2 << 30, bytes_accessed=4 << 20, transcendentals=0),
        name="multiples",
    )(selected, traces, live, jnp.asarray(fwd), jnp.asarray(inv))
    return out.transpose(1, 0, 2)[:, None]


def solution(mesh):
    in_specs = (P("af", "row", None), P("af", "row"), P())
    out_specs = P(None, "row", "af", None)
    return jax.shard_map(per_device, mesh=mesh, in_specs=in_specs, out_specs=out_specs, check_vma=False)
```

```python
import functools
import math

import jax
import jax.numpy as jnp
import numpy as np
from jax import lax
from jax.experimental import pallas as pl
from jax.experimental.pallas import tpu as pltpu
from jax.sharding import PartitionSpec as P

MESH = pl.DeviceIdType.MESH
BF, F32, I32 = jnp.bfloat16, jnp.float32, jnp.int32

NX, NY, NZ, NROW = 4, 8, 4, 4
NT, NF, SHOTS, RECV, OUT = 512, 256, 8, 256, 32
BANDS, PER = 32, 8
COMP = 2 * PER
GROUPS = 2
PER_G = PER // GROUPS


def host_tables():
    t = np.arange(NT)[:, None]
    f = np.arange(NF)[None, :]
    ang = (t * f % NT) * (2.0 * math.pi / NT)
    norm = 1.0 / math.sqrt(NT)
    w = np.where(np.arange(NF) == 0, 1.0, 2.0)[:, None]
    cos, sin = np.cos(ang).T, -np.sin(ang).T
    fwd = np.stack([cos.reshape(BANDS, PER, NT), sin.reshape(BANDS, PER, NT)], axis=1) * norm
    inv = np.concatenate([cos * w, sin * w], axis=0) * norm
    as_bf = lambda a: a.astype(np.float32).astype(jnp.bfloat16)
    fwd = fwd.reshape(2 * NF, NT)
    return as_bf(np.concatenate([fwd, fwd[:128]])), as_bf(inv)


def af(x, y, z):
    return (x * NY + y) * NZ + z


def base_of(y):
    return lax.rem(y - 2 + lax.rem(y, 2) + NY, NY)


def iota(shape, dim):
    return lax.broadcasted_iota(I32, shape, dim)


def mm(a, b, dims=((1,), (0,))):
    return lax.dot_general(a, b, (dims, ((), ())), preferred_element_type=F32)


def kernel(
    phases, sel_hbm, traces_hbm, live_hbm, fwd_hbm, inv_hbm, out_ref,
    sel_ref, live_ref, traces, fwd, inv, send, recv, bt, perm, pick, lanes, spread,
    a_own, a_msg, a_in, a_row, p2, stage, r_send, r_recv,
    load_sem, send_sem, recv_sem, own_sem, a_send_sem, a_recv_sem, row_send_sem, row_recv_sem,
    r_send_sem, r_recv_sem, r_own_sem,
):
    per_phase = SHOTS // phases
    joined = 16 // per_phase
    blocks = 8 // joined
    run = 64 // phases

    a = lax.axis_index("af")
    row = lax.axis_index("row")
    x, y, z = lax.div(a, NY * NZ), lax.rem(lax.div(a, NZ), NY), lax.rem(a, NZ)
    half, zp, zs, odd = lax.div(y, 2), lax.div(z, 2), lax.rem(z, 2), lax.rem(y, 2)
    base = base_of(y)
    xs = [lax.rem(x + i, NX) for i in range(NX)]
    ys = [lax.rem(y + i, NY) for i in range(NY)]
    zz = [lax.rem(z + i, NZ) for i in range(NZ)]
    other = lax.rem(row + 2, NROW)
    cores = (a, row + 1 - 2 * lax.rem(row, 2))
    across = (a, other)
    pair = [z, z + 1 - 2 * zs]
    to_y = [lax.rem(2 * half - 1 + lax.rem(odd + 1 + w, 4) + NY, NY) for w in range(4)]
    from_y = [lax.rem(base + lax.rem(lax.rem(y - base + NY, NY) + w, 4), NY) for w in range(4)]
    homes = [af(x, ys[4 * (u // 2)], zz[2 * (u % 2)]) for u in range(4)]

    fwd_copy = pltpu.make_async_copy(fwd_hbm, fwd, load_sem.at[SHOTS])
    inv_copy = pltpu.make_async_copy(inv_hbm, inv, load_sem.at[SHOTS + 1])
    live_copy = pltpu.make_async_copy(live_hbm, live_ref, load_sem.at[SHOTS + 2])
    sel_copy = pltpu.make_async_copy(sel_hbm, sel_ref, load_sem.at[SHOTS + 3])
    sel_copy.start()
    fwd_copy.start()
    live_copy.start()
    loads = [pltpu.make_async_copy(traces_hbm.at[s], traces.at[s], load_sem.at[s]) for s in range(SHOTS)]
    for c in loads:
        c.start()
    inv_copy.start()

    barrier = pltpu.get_barrier_semaphore()

    for i in range(1, BANDS):
        pl.semaphore_signal(
            barrier, inc=1, device_id=(af(xs[i // 8], from_y[i // 2 % 4], pair[i % 2]), row), device_id_type=MESH
        )
    for u in range(1, 4):
        pl.semaphore_signal(barrier, inc=1, device_id=(homes[u], row), device_id_type=MESH)
    pl.semaphore_signal(barrier, inc=1, device_id=cores, device_id_type=MESH)
    pl.semaphore_signal(barrier, inc=1, device_id=across, device_id_type=MESH)

    sel_copy.wait()
    chosen = [sel_ref[o] - a * SHOTS for o in range(OUT)]
    flag = [sum((c == s).astype(I32) for c in chosen) for s in range(SHOTS)]
    count = sum(flag)
    place, ahead = [], 0
    for s in range(SHOTS):
        place.append(jnp.where(flag[s] > 0, ahead, count + s - ahead))
        ahead = ahead + flag[s]
    shot_at = [sum(jnp.where(place[s] == n, s, 0) for s in range(SHOTS)) for n in range(SHOTS)]

    fwd_copy.wait()
    live_copy.wait()
    for c in loads:
        c.wait()

    def band_of(bx, hy, hz):
        return bx * 8 + lax.rem(hy, 4) * 2 + lax.rem(hz, 2)

    to_slot = [x * 8 + lax.rem(y - base_of(hy) + NY, NY) * 2 + zs for hy in to_y]

    def band_copy(ph, dx, w, dz):
        band, slot = band_of(xs[dx], to_y[w], pair[dz]), to_slot[w]
        return pltpu.make_async_remote_copy(
            src_ref=send.at[ph, band], dst_ref=recv.at[ph, slot],
            send_sem=send_sem.at[(dx * 4 + w) * 2 + dz if ph < phases - 1 else 0],
            recv_sem=recv_sem.at[ph, slot], device_id=(af(xs[dx], to_y[w], pair[dz]), row), device_id_type=MESH,
        )

    own_band, own_slot = band_of(x, y, z), to_slot[0]
    own_copies = [
        pltpu.make_async_copy(send.at[ph, own_band], recv.at[ph, own_slot], own_sem.at[ph]) for ph in range(phases)
    ]
    order = [
        [((1 + 2 * i + j % 2) % NX, (j // 2 + 1) % 4, (j // 8 + 1) % 2) for j in range(16)] for i in range(2)
    ]
    order = [[t for t in part if t != (0, 0, 0)] for part in order]

    for ph in range(phases):
        for i in range(2):
            first = xs[(1 + 2 * i) % NX]
            second = xs[(2 + 2 * i) % NX]
            table = fwd[pl.ds(pl.multiple_of(first * 128, 128), 256), :]
            for n in range(per_phase):
                shot = shot_at[ph * per_phase + n]
                spec = mm(table, traces[shot], ((1,), (1,))) * live_ref[pl.ds(shot, 1), :].astype(F32)
                spec = spec.astype(BF).reshape(2, 8, COMP, RECV)
                send[ph, pl.ds(first * 8, 8), n] = spec[0]
                send[ph, pl.ds(second * 8, 8), n] = spec[1]
            if ph == 0:
                if i == 0:
                    pl.semaphore_wait(barrier, BANDS - 1 + 3 + 2)
                for t in order[i]:
                    band_copy(0, *t).start()
        own_copies[ph].start()

    ro, co = iota((256, 256), 0), iota((256, 256), 1)
    perm[...] = jnp.where(co == ro % 16 * 16 + ro // 16, 1.0, 0.0).astype(BF)
    col = jnp.full((OUT, 128), -1, I32)
    line = jnp.full((1, 128), -1, I32)
    for o in range(OUT):
        col = jnp.where(iota((OUT, 128), 0) == o, sel_ref[o], col)
        line = jnp.where(iota((1, 128), 1) == o, sel_ref[o], line)
    before = (line // SHOTS == col // SHOTS) & (line < col) & (iota((OUT, 128), 1) < OUT)
    rank = jnp.sum(jnp.where(before, 1.0, 0.0), axis=1, keepdims=True).astype(I32)
    want = col[:, 0:1] // SHOTS * SHOTS + rank
    j = iota((1, 512 // phases), 1)
    k = j % run
    src, place_k = k // per_phase, k % per_phase
    part = j // run % 2
    device = (j // (2 * run) * NY + (base + src // 2) % NY) * NZ + 2 * zp + src % 2
    hit = want == device * SHOTS + place_k
    pick[0:OUT, :] = jnp.where(hit & (part == 0), 1.0, 0.0).astype(BF)
    pick[OUT : 2 * OUT, :] = jnp.where(hit & (part == 1), 1.0, 0.0).astype(BF)
    r_at = iota((256, 128), 0)
    here = jnp.where((row * RECV + r_at == line) & (iota((256, 128), 1) < OUT), 1.0, 0.0)
    same = ro // SHOTS == co // SHOTS
    ahead_of = mm(jnp.where(same & (co < ro), 1.0, 0.0).astype(BF), here.astype(BF))
    all_of = mm(jnp.where(same, 1.0, 0.0).astype(BF), here.astype(BF))
    total_of = lambda v: jnp.sum(v, axis=1, keepdims=True).astype(I32)
    n_here, n_ahead, n_all = total_of(here), total_of(ahead_of), total_of(all_of)
    r1 = iota((256, 1), 0)
    at = jnp.where(n_here > 0, n_ahead, n_all + r1 % SHOTS - n_ahead)
    ry, rz = (r1 // (NZ * SHOTS) - base + NY) % NY, r1 // SHOTS % NZ
    u = ry // 4 * 2 + jnp.where(rz // 2 == zp, 0, 1)
    to = u * 128 + at // per_phase * (2 * run) + (ry % 4 * 2 + rz % 2) * per_phase + at % per_phase
    for p in range(2):
        lanes[p * 256 : (p + 1) * 256, :] = jnp.where(iota((256, 512), 1) == to + p * run, 1.0, 0.0).astype(BF)
    d_at = iota((128, 512), 0)
    j2 = iota((128, 512), 1)
    spread[...] = jnp.where(j2 % 256 == 2 * d_at + j2 // 256, 1.0, 0.0).astype(BF)
    p2[...] = jnp.zeros_like(p2)

    for i in range(2):
        for t in order[i]:
            if phases == 2:
                band_copy(0, *t).wait_send()
                band_copy(1, *t).start()

    def arrive(ph, start, stop):
        @pl.loop(start, stop)
        def _(i):
            sx = lax.rem(x + 2 * NX - 1 - i, NX)
            for q in range(8):
                slot = sx * 8 + q

                @pl.when(slot != own_slot)
                def _():
                    pltpu.make_async_remote_copy(
                        src_ref=send.at[ph, 0], dst_ref=recv.at[ph, slot], send_sem=send_sem.at[0],
                        recv_sem=recv_sem.at[ph, slot], device_id=cores, device_id_type=MESH,
                    ).wait_recv()

            for q in range(blocks):
                block = recv[ph, pl.ds(sx * 8 + q * joined, joined)].reshape(256, RECV)
                turned = mm(perm[...], block).astype(BF).reshape(2, PER, 16, RECV)
                bt[:, sx, ph, 0, q] = turned[0]
                bt[:, sx, ph, 1, q] = turned[1]

    for c in own_copies:
        c.wait()
    arrive(0, 0, NX)

    def home_copy(g, v):
        return pltpu.make_async_remote_copy(
            src_ref=a_msg.at[g, v], dst_ref=a_in.at[g, v], send_sem=a_send_sem.at[g, v],
            recv_sem=a_recv_sem.at[g, v], device_id=(homes[v], row), device_id_type=MESH,
        )

    def row_copy(g, slot, to, sem):
        return pltpu.make_async_remote_copy(
            src_ref=a_row.at[slot, g], dst_ref=a_row.at[slot, g], send_sem=row_send_sem.at[g, sem],
            recv_sem=row_recv_sem.at[g, sem], device_id=to, device_id_type=MESH,
        )

    for g in range(GROUPS):
        for f in range(PER_G):
            got = mm(pick[...], bt[g * PER_G + f, :, 0].reshape(512 // phases, RECV)).astype(BF)
            a_own[g, f * OUT : (f + 1) * OUT, 0:RECV] = got[0:OUT]
            a_own[g, f * OUT : (f + 1) * OUT, RECV:] = got[OUT:]
        for v in (3, 2, 1, 0):
            a_msg[g, v] = mm(a_own[g], lanes[:, v * 128 : (v + 1) * 128]).astype(BF)
            if v:
                home_copy(g, v).start()

    to_across = [row_copy(g, row, across, 0) for g in range(GROUPS)]
    to_core = [row_copy(g, row, cores, 1) for g in range(GROUPS)]
    onward = [row_copy(g, other, cores, 2) for g in range(GROUPS)]
    for g in range(GROUPS):
        for v in (1, 2, 3):
            home_copy(g, v).wait()
        a_row[row, g] = a_msg[g, 0] + a_in[g, 1] + a_in[g, 2] + a_in[g, 3]
        to_across[g].start()
        to_core[g].start()
    if phases == 2:
        arrive(1, 0, 2)
    for g in range(GROUPS):
        to_across[g].wait_recv()
        onward[g].start()
    if phases == 2:
        arrive(1, 2, NX)

    imag = iota((1, 128), 1) // run % 2 == 1
    sign = jnp.where(imag, -1.0, 1.0)
    factor = 1.0 / math.sqrt(NX * NY * NZ * SHOTS)
    for g in range(GROUPS):
        to_core[g].wait_recv()
        onward[g].wait_recv()
        left = []
        for v in range(NROW):
            val = a_row[v, g].astype(F32)
            swapped = jnp.where(imag, pltpu.roll(val, run, 1), pltpu.roll(val, 128 - run, 1))
            left.append(((val * sign).astype(BF), swapped.astype(BF)))
        for f in range(PER_G):
            rows = slice(f * OUT, (f + 1) * OUT)
            lhs = jnp.concatenate(
                [jnp.concatenate([left[v][p][rows] for v in range(NROW)], axis=1) for p in range(2)], axis=0
            )
            at = g * PER_G + f
            pred = (mm(lhs, bt[at].reshape(512, RECV)) * factor).astype(BF)
            p2[at, 0:64, 0:RECV] = pred
            p2[at, 64:128, RECV:] = pred

    for f in range(PER):
        stage[pl.ds(f, 128, stride=8), :] = mm(spread[...], p2[f], ((1,), (1,)))
    r_send[...] = stage[...].astype(BF).reshape(128, 8, 128)

    my_slot = (lax.div(y, 4) * 2 + zp) * BANDS + own_band
    own_r = pltpu.make_async_copy(r_send.at[a], r_recv.at[my_slot], r_own_sem)
    own_r.start()

    def back(d):
        pltpu.make_async_remote_copy(
            src_ref=r_send.at[d], dst_ref=r_recv.at[my_slot], send_sem=r_send_sem,
            recv_sem=r_recv_sem, device_id=(d, row), device_id_type=MESH,
        ).start()

    @pl.loop(0, NY)
    def _(i):
        dy = lax.rem(y + 4 + i, NY)
        for j in range(1, 16):
            back(af(xs[j % NX], dy, zz[j // NX]))

        @pl.when(i != 4)
        def _():
            back(af(x, dy, z))

    all_r = pltpu.make_async_remote_copy(
        src_ref=r_send.at[pl.ds(0, 127)], dst_ref=r_recv.at[pl.ds(0, 127)], send_sem=r_send_sem,
        recv_sem=r_recv_sem, device_id=cores, device_id_type=MESH,
    )
    inv_copy.wait()
    own_r.wait()
    all_r.wait_recv()

    total = r_recv[0:32].astype(F32)
    for v in range(1, 4):
        total = total + r_recv[v * 32 : (v + 1) * 32].astype(F32)
    turned = total.reshape(256, 128).T.astype(BF)
    lhs = jnp.concatenate(
        [jnp.concatenate([turned[r * 64 : r * 64 + 32], turned[r * 64 + 32 : r * 64 + 64]], axis=1) for r in range(2)],
        axis=0,
    )
    res = mm(lhs, inv[...])
    for r in range(2):
        out_ref[r] = res[r * 32 : (r + 1) * 32]

    all_r.wait_send()
    for g in range(GROUPS):
        for c in (to_across[g], to_core[g], onward[g]):
            c.wait_send()
    pltpu.make_async_remote_copy(
        src_ref=send.at[phases - 1, pl.ds(0, 31)], dst_ref=recv.at[phases - 1, pl.ds(0, 31)],
        send_sem=send_sem.at[0], recv_sem=recv_sem.at[0, 0], device_id=cores, device_id_type=MESH,
    ).wait_send()


def per_device(traces, live, selected):
    fwd, inv = host_tables()
    any_, vmem = pl.BlockSpec(memory_space=pl.ANY), pl.BlockSpec(memory_space=pltpu.VMEM)
    dma = pltpu.SemaphoreType.DMA

    def call(phases):
        per_phase, blocks = SHOTS // phases, SHOTS * SHOTS // 16 // phases
        return pl.pallas_call(
            functools.partial(kernel, phases),
            out_shape=jax.ShapeDtypeStruct((2, OUT, NT), F32),
            in_specs=[any_] * 5,
            out_specs=vmem,
            scratch_shapes=[
                pltpu.SMEM((OUT,), I32),
                pltpu.VMEM((SHOTS, RECV), I32),
                pltpu.VMEM((SHOTS, RECV, NT), BF),
                pltpu.VMEM((2 * NF + 128, NT), BF),
                pltpu.VMEM((2 * NF, NT), BF),
                pltpu.VMEM((phases, BANDS, per_phase, COMP, RECV), BF),
                pltpu.VMEM((phases, BANDS, per_phase, COMP, RECV), BF),
                pltpu.VMEM((PER, NX, phases, 2, blocks, 16, RECV), BF),
                pltpu.VMEM((256, 256), BF),
                pltpu.VMEM((2 * OUT, 512 // phases), BF),
                pltpu.VMEM((512, 512), BF),
                pltpu.VMEM((128, 512), BF),
                pltpu.VMEM((GROUPS, PER_G * OUT, 512), BF),
                pltpu.VMEM((GROUPS, 4, PER_G * OUT, 128), BF),
                pltpu.VMEM((GROUPS, 4, PER_G * OUT, 128), BF),
                pltpu.VMEM((NROW, GROUPS, PER_G * OUT, 128), BF),
                pltpu.VMEM((PER, 128, 512), BF),
                pltpu.VMEM((1024, 128), F32),
                pltpu.VMEM((128, 8, 128), BF),
                pltpu.VMEM((128, 8, 128), BF),
                dma((SHOTS + 4,)), dma((BANDS,)), dma((phases, BANDS)), dma((phases,)),
                dma((GROUPS, 4)), dma((GROUPS, 4)), dma((GROUPS, 3)), dma((GROUPS, 3)),
                dma, dma, dma,
            ],
            compiler_params=pltpu.CompilerParams(
                collective_id=phases, has_side_effects=True, vmem_limit_bytes=60 << 20
            ),
            cost_estimate=pl.CostEstimate(flops=2 << 30, bytes_accessed=4 << 20, transcendentals=0),
            name="multiples",
        )(selected, traces, live, jnp.asarray(fwd), jnp.asarray(inv))

    owner = selected // SHOTS
    most = jnp.max(jnp.sum((owner[:, None] == owner[None, :]).astype(I32), axis=1))
    out = lax.cond(most <= SHOTS // 2, lambda: call(2), lambda: call(1))
    return out.transpose(1, 0, 2)[:, None]


def solution(mesh):
    in_specs = (P("af", "row", None), P("af", "row"), P())
    out_specs = P(None, "row", "af", None)
    return jax.shard_map(per_device, mesh=mesh, in_specs=in_specs, out_specs=out_specs, check_vma=False)
```

```python
import functools
import math

import jax
import jax.numpy as jnp
import numpy as np
from jax import lax
from jax.experimental import pallas as pl
from jax.experimental.pallas import tpu as pltpu
from jax.sharding import PartitionSpec as P

MESH = pl.DeviceIdType.MESH
BF, F32, I32 = jnp.bfloat16, jnp.float32, jnp.int32

NX, NY, NZ, NROW = 4, 8, 4, 4
NT, NF, SHOTS, RECV, OUT = 512, 256, 8, 256, 32
BANDS, PER = 32, 8
COMP = 2 * PER
GROUPS = 2
PER_G = PER // GROUPS
METER = (8, 18, 31)


def host_tables():
    t = np.arange(NT)[:, None]
    f = np.arange(NF)[None, :]
    ang = (t * f % NT) * (2.0 * math.pi / NT)
    norm = 1.0 / math.sqrt(NT)
    w = np.where(np.arange(NF) == 0, 1.0, 2.0)[:, None]
    cos, sin = np.cos(ang).T, -np.sin(ang).T
    fwd = np.stack([cos.reshape(BANDS, PER, NT), sin.reshape(BANDS, PER, NT)], axis=1) * norm
    inv = np.concatenate([cos * w, sin * w], axis=0) * norm
    as_bf = lambda a: a.astype(np.float32).astype(jnp.bfloat16)
    fwd = fwd.reshape(2 * NF, NT)
    return as_bf(np.concatenate([fwd, fwd[:128]])), as_bf(inv)


def af(x, y, z):
    return (x * NY + y) * NZ + z


def base_of(y):
    return lax.rem(y - 2 + lax.rem(y, 2) + NY, NY)


def iota(shape, dim):
    return lax.broadcasted_iota(I32, shape, dim)


def mm(a, b, dims=((1,), (0,))):
    return lax.dot_general(a, b, (dims, ((), ())), preferred_element_type=F32)


def kernel(
    phases, sel_hbm, traces_hbm, live_hbm, fwd_hbm, inv_hbm, out_ref,
    sel_ref, live_ref, traces, fwd, inv, send, recv, bt, perm, pick, lanes, spread,
    a_own, a_msg, a_in, a_row, p2, stage, r_send, r_recv,
    load_sem, send_sem, recv_sem, own_sem, a_send_sem, a_recv_sem, row_send_sem, row_recv_sem,
    r_send_sem, r_recv_sem, r_own_sem,
):
    per_phase = SHOTS // phases
    joined = 16 // per_phase
    blocks = 8 // joined
    run = 64 // phases

    a = lax.axis_index("af")
    row = lax.axis_index("row")
    x, y, z = lax.div(a, NY * NZ), lax.rem(lax.div(a, NZ), NY), lax.rem(a, NZ)
    half, zp, zs, odd = lax.div(y, 2), lax.div(z, 2), lax.rem(z, 2), lax.rem(y, 2)
    base = base_of(y)
    xs = [lax.rem(x + i, NX) for i in range(NX)]
    ys = [lax.rem(y + i, NY) for i in range(NY)]
    zz = [lax.rem(z + i, NZ) for i in range(NZ)]
    other = lax.rem(row + 2, NROW)
    cores = (a, row + 1 - 2 * lax.rem(row, 2))
    across = (a, other)
    pair = [z, z + 1 - 2 * zs]
    to_y = [lax.rem(2 * half - 1 + lax.rem(odd + 1 + w, 4) + NY, NY) for w in range(4)]
    from_y = [lax.rem(base + lax.rem(lax.rem(y - base + NY, NY) + w, 4), NY) for w in range(4)]
    homes = [af(x, ys[4 * (u // 2)], zz[2 * (u % 2)]) for u in range(4)]

    fwd_copy = pltpu.make_async_copy(fwd_hbm, fwd, load_sem.at[SHOTS])
    inv_copy = pltpu.make_async_copy(inv_hbm, inv, load_sem.at[SHOTS + 1])
    live_copy = pltpu.make_async_copy(live_hbm, live_ref, load_sem.at[SHOTS + 2])
    sel_copy = pltpu.make_async_copy(sel_hbm, sel_ref, load_sem.at[SHOTS + 3])
    sel_copy.start()
    fwd_copy.start()
    live_copy.start()
    loads = [pltpu.make_async_copy(traces_hbm.at[s], traces.at[s], load_sem.at[s]) for s in range(SHOTS)]
    for c in loads:
        c.start()
    inv_copy.start()

    barrier = pltpu.get_barrier_semaphore()

    for i in range(1, BANDS):
        pl.semaphore_signal(
            barrier, inc=1, device_id=(af(xs[i // 8], from_y[i // 2 % 4], pair[i % 2]), row), device_id_type=MESH
        )
    for u in range(1, 4):
        pl.semaphore_signal(barrier, inc=1, device_id=(homes[u], row), device_id_type=MESH)
    pl.semaphore_signal(barrier, inc=1, device_id=cores, device_id_type=MESH)
    pl.semaphore_signal(barrier, inc=1, device_id=across, device_id_type=MESH)

    sel_copy.wait()
    chosen = [sel_ref[o] - a * SHOTS for o in range(OUT)]
    flag = [sum((c == s).astype(I32) for c in chosen) for s in range(SHOTS)]
    count = sum(flag)
    place, ahead = [], 0
    for s in range(SHOTS):
        place.append(jnp.where(flag[s] > 0, ahead, count + s - ahead))
        ahead = ahead + flag[s]
    shot_at = [sum(jnp.where(place[s] == n, s, 0) for s in range(SHOTS)) for n in range(SHOTS)]

    fwd_copy.wait()
    live_copy.wait()
    for c in loads:
        c.wait()

    def band_of(bx, hy, hz):
        return bx * 8 + lax.rem(hy, 4) * 2 + lax.rem(hz, 2)

    to_slot = [x * 8 + lax.rem(y - base_of(hy) + NY, NY) * 2 + zs for hy in to_y]

    def band_copy(ph, dx, w, dz):
        band, slot = band_of(xs[dx], to_y[w], pair[dz]), to_slot[w]
        return pltpu.make_async_remote_copy(
            src_ref=send.at[ph, band], dst_ref=recv.at[ph, slot],
            send_sem=send_sem.at[(dx * 4 + w) * 2 + dz if ph < phases - 1 else 0],
            recv_sem=recv_sem.at[ph, slot], device_id=(af(xs[dx], to_y[w], pair[dz]), row), device_id_type=MESH,
        )

    own_band, own_slot = band_of(x, y, z), to_slot[0]
    own_copies = [
        pltpu.make_async_copy(send.at[ph, own_band], recv.at[ph, own_slot], own_sem.at[ph]) for ph in range(phases)
    ]
    order = [
        [((1 + 2 * i + j % 2) % NX, (j // 2 + 1) % 4, (j // 8 + 1) % 2) for j in range(16)] for i in range(2)
    ]
    order = [[t for t in part if t != (0, 0, 0)] for part in order]

    for ph in range(phases):
        for i in range(2):
            first = xs[(1 + 2 * i) % NX]
            second = xs[(2 + 2 * i) % NX]
            table = fwd[pl.ds(pl.multiple_of(first * 128, 128), 256), :]
            for n in range(per_phase):
                shot = shot_at[ph * per_phase + n]
                spec = mm(table, traces[shot], ((1,), (1,))) * live_ref[pl.ds(shot, 1), :].astype(F32)
                spec = spec.astype(BF).reshape(2, 8, COMP, RECV)
                send[ph, pl.ds(first * 8, 8), n] = spec[0]
                send[ph, pl.ds(second * 8, 8), n] = spec[1]
            if ph == 0:
                if i == 0:
                    pl.semaphore_wait(barrier, BANDS - 1 + 3 + 2)
                for t in order[i]:
                    band_copy(0, *t).start()
        own_copies[ph].start()

    ro, co = iota((256, 256), 0), iota((256, 256), 1)
    perm[...] = jnp.where(co == ro % 16 * 16 + ro // 16, 1.0, 0.0).astype(BF)
    col = jnp.full((OUT, 128), -1, I32)
    line = jnp.full((1, 128), -1, I32)
    for o in range(OUT):
        col = jnp.where(iota((OUT, 128), 0) == o, sel_ref[o], col)
        line = jnp.where(iota((1, 128), 1) == o, sel_ref[o], line)
    before = (line // SHOTS == col // SHOTS) & (line < col) & (iota((OUT, 128), 1) < OUT)
    rank = jnp.sum(jnp.where(before, 1.0, 0.0), axis=1, keepdims=True).astype(I32)
    want = col[:, 0:1] // SHOTS * SHOTS + rank
    j = iota((1, 512 // phases), 1)
    k = j % run
    src, place_k = k // per_phase, k % per_phase
    part = j // run % 2
    device = (j // (2 * run) * NY + (base + src // 2) % NY) * NZ + 2 * zp + src % 2
    hit = want == device * SHOTS + place_k
    pick[0:OUT, :] = jnp.where(hit & (part == 0), 1.0, 0.0).astype(BF)
    pick[OUT : 2 * OUT, :] = jnp.where(hit & (part == 1), 1.0, 0.0).astype(BF)
    r_at = iota((256, 128), 0)
    here = jnp.where((row * RECV + r_at == line) & (iota((256, 128), 1) < OUT), 1.0, 0.0)
    same = ro // SHOTS == co // SHOTS
    ahead_of = mm(jnp.where(same & (co < ro), 1.0, 0.0).astype(BF), here.astype(BF))
    all_of = mm(jnp.where(same, 1.0, 0.0).astype(BF), here.astype(BF))
    total_of = lambda v: jnp.sum(v, axis=1, keepdims=True).astype(I32)
    n_here, n_ahead, n_all = total_of(here), total_of(ahead_of), total_of(all_of)
    r1 = iota((256, 1), 0)
    at = jnp.where(n_here > 0, n_ahead, n_all + r1 % SHOTS - n_ahead)
    ry, rz = (r1 // (NZ * SHOTS) - base + NY) % NY, r1 // SHOTS % NZ
    u = ry // 4 * 2 + jnp.where(rz // 2 == zp, 0, 1)
    to = u * 128 + at // per_phase * (2 * run) + (ry % 4 * 2 + rz % 2) * per_phase + at % per_phase
    for p in range(2):
        lanes[p * 256 : (p + 1) * 256, :] = jnp.where(iota((256, 512), 1) == to + p * run, 1.0, 0.0).astype(BF)
    d_at = iota((128, 512), 0)
    j2 = iota((128, 512), 1)
    spread[...] = jnp.where(j2 % 256 == 2 * d_at + j2 // 256, 1.0, 0.0).astype(BF)
    p2[...] = jnp.zeros_like(p2)

    def second_phase(start, stop):
        for t in (order[0] + order[1])[start:stop] if phases == 2 else ():
            band_copy(0, *t).wait_send()
            band_copy(1, *t).start()

    second_phase(0, METER[0])

    def arrive(ph, start, stop):
        @pl.loop(start, stop)
        def _(i):
            sx = lax.rem(x + 2 * NX - 1 - i, NX)
            for q in range(8):
                slot = sx * 8 + q

                @pl.when(slot != own_slot)
                def _():
                    pltpu.make_async_remote_copy(
                        src_ref=send.at[ph, 0], dst_ref=recv.at[ph, slot], send_sem=send_sem.at[0],
                        recv_sem=recv_sem.at[ph, slot], device_id=cores, device_id_type=MESH,
                    ).wait_recv()

            for q in range(blocks):
                block = recv[ph, pl.ds(sx * 8 + q * joined, joined)].reshape(256, RECV)
                turned = mm(perm[...], block).astype(BF).reshape(2, PER, 16, RECV)
                bt[:, sx, ph, 0, q] = turned[0]
                bt[:, sx, ph, 1, q] = turned[1]

    for c in own_copies:
        c.wait()
    arrive(0, 0, NX)

    def home_copy(g, v):
        return pltpu.make_async_remote_copy(
            src_ref=a_msg.at[g, v], dst_ref=a_in.at[g, v], send_sem=a_send_sem.at[g, v],
            recv_sem=a_recv_sem.at[g, v], device_id=(homes[v], row), device_id_type=MESH,
        )

    def row_copy(g, slot, to, sem):
        return pltpu.make_async_remote_copy(
            src_ref=a_row.at[slot, g], dst_ref=a_row.at[slot, g], send_sem=row_send_sem.at[g, sem],
            recv_sem=row_recv_sem.at[g, sem], device_id=to, device_id_type=MESH,
        )

    for g in range(GROUPS):
        for f in range(PER_G):
            got = mm(pick[...], bt[g * PER_G + f, :, 0].reshape(512 // phases, RECV)).astype(BF)
            a_own[g, f * OUT : (f + 1) * OUT, 0:RECV] = got[0:OUT]
            a_own[g, f * OUT : (f + 1) * OUT, RECV:] = got[OUT:]
        for v in (3, 2, 1, 0):
            a_msg[g, v] = mm(a_own[g], lanes[:, v * 128 : (v + 1) * 128]).astype(BF)
            if v:
                home_copy(g, v).start()

    second_phase(METER[0], METER[1])

    to_across = [row_copy(g, row, across, 0) for g in range(GROUPS)]
    to_core = [row_copy(g, row, cores, 1) for g in range(GROUPS)]
    onward = [row_copy(g, other, cores, 2) for g in range(GROUPS)]
    for g in range(GROUPS):
        for v in (1, 2, 3):
            home_copy(g, v).wait()
        a_row[row, g] = a_msg[g, 0] + a_in[g, 1] + a_in[g, 2] + a_in[g, 3]
        to_across[g].start()
        to_core[g].start()
    second_phase(METER[1], METER[2])
    if phases == 2:
        arrive(1, 0, 2)
    for g in range(GROUPS):
        to_across[g].wait_recv()
        onward[g].start()
    second_phase(METER[2], BANDS)
    if phases == 2:
        arrive(1, 2, NX)

    imag = iota((1, 128), 1) // run % 2 == 1
    sign = jnp.where(imag, -1.0, 1.0)
    factor = 1.0 / math.sqrt(NX * NY * NZ * SHOTS)
    for g in range(GROUPS):
        to_core[g].wait_recv()
        onward[g].wait_recv()
        left = []
        for v in range(NROW):
            val = a_row[v, g].astype(F32)
            swapped = jnp.where(imag, pltpu.roll(val, run, 1), pltpu.roll(val, 128 - run, 1))
            left.append(((val * sign).astype(BF), swapped.astype(BF)))
        for f in range(PER_G):
            rows = slice(f * OUT, (f + 1) * OUT)
            lhs = jnp.concatenate(
                [jnp.concatenate([left[v][p][rows] for v in range(NROW)], axis=1) for p in range(2)], axis=0
            )
            at = g * PER_G + f
            pred = (mm(lhs, bt[at].reshape(512, RECV)) * factor).astype(BF)
            p2[at, 0:64, 0:RECV] = pred
            p2[at, 64:128, RECV:] = pred

    for f in range(PER):
        stage[pl.ds(f, 128, stride=8), :] = mm(spread[...], p2[f], ((1,), (1,)))
    r_send[...] = stage[...].astype(BF).reshape(128, 8, 128)

    my_slot = (lax.div(y, 4) * 2 + zp) * BANDS + own_band
    own_r = pltpu.make_async_copy(r_send.at[a], r_recv.at[my_slot], r_own_sem)
    own_r.start()

    def back(d):
        pltpu.make_async_remote_copy(
            src_ref=r_send.at[d], dst_ref=r_recv.at[my_slot], send_sem=r_send_sem,
            recv_sem=r_recv_sem, device_id=(d, row), device_id_type=MESH,
        ).start()

    @pl.loop(0, NY)
    def _(i):
        dy = lax.rem(y + 4 + i, NY)
        for j in range(1, 16):
            back(af(xs[j % NX], dy, zz[j // NX]))

        @pl.when(i != 4)
        def _():
            back(af(x, dy, z))

    all_r = pltpu.make_async_remote_copy(
        src_ref=r_send.at[pl.ds(0, 127)], dst_ref=r_recv.at[pl.ds(0, 127)], send_sem=r_send_sem,
        recv_sem=r_recv_sem, device_id=cores, device_id_type=MESH,
    )
    inv_copy.wait()
    own_r.wait()
    all_r.wait_recv()

    total = r_recv[0:32].astype(F32)
    for v in range(1, 4):
        total = total + r_recv[v * 32 : (v + 1) * 32].astype(F32)
    turned = total.reshape(256, 128).T.astype(BF)
    lhs = jnp.concatenate(
        [jnp.concatenate([turned[r * 64 : r * 64 + 32], turned[r * 64 + 32 : r * 64 + 64]], axis=1) for r in range(2)],
        axis=0,
    )
    res = mm(lhs, inv[...])
    for r in range(2):
        out_ref[r] = res[r * 32 : (r + 1) * 32]

    all_r.wait_send()
    for g in range(GROUPS):
        for c in (to_across[g], to_core[g], onward[g]):
            c.wait_send()
    pltpu.make_async_remote_copy(
        src_ref=send.at[phases - 1, pl.ds(0, 31)], dst_ref=recv.at[phases - 1, pl.ds(0, 31)],
        send_sem=send_sem.at[0], recv_sem=recv_sem.at[0, 0], device_id=cores, device_id_type=MESH,
    ).wait_send()


def per_device(traces, live, selected):
    fwd, inv = host_tables()
    any_, vmem = pl.BlockSpec(memory_space=pl.ANY), pl.BlockSpec(memory_space=pltpu.VMEM)
    dma = pltpu.SemaphoreType.DMA

    def call(phases):
        per_phase, blocks = SHOTS // phases, SHOTS * SHOTS // 16 // phases
        return pl.pallas_call(
            functools.partial(kernel, phases),
            out_shape=jax.ShapeDtypeStruct((2, OUT, NT), F32),
            in_specs=[any_] * 5,
            out_specs=vmem,
            scratch_shapes=[
                pltpu.SMEM((OUT,), I32),
                pltpu.VMEM((SHOTS, RECV), I32),
                pltpu.VMEM((SHOTS, RECV, NT), BF),
                pltpu.VMEM((2 * NF + 128, NT), BF),
                pltpu.VMEM((2 * NF, NT), BF),
                pltpu.VMEM((phases, BANDS, per_phase, COMP, RECV), BF),
                pltpu.VMEM((phases, BANDS, per_phase, COMP, RECV), BF),
                pltpu.VMEM((PER, NX, phases, 2, blocks, 16, RECV), BF),
                pltpu.VMEM((256, 256), BF),
                pltpu.VMEM((2 * OUT, 512 // phases), BF),
                pltpu.VMEM((512, 512), BF),
                pltpu.VMEM((128, 512), BF),
                pltpu.VMEM((GROUPS, PER_G * OUT, 512), BF),
                pltpu.VMEM((GROUPS, 4, PER_G * OUT, 128), BF),
                pltpu.VMEM((GROUPS, 4, PER_G * OUT, 128), BF),
                pltpu.VMEM((NROW, GROUPS, PER_G * OUT, 128), BF),
                pltpu.VMEM((PER, 128, 512), BF),
                pltpu.VMEM((1024, 128), F32),
                pltpu.VMEM((128, 8, 128), BF),
                pltpu.VMEM((128, 8, 128), BF),
                dma((SHOTS + 4,)), dma((BANDS,)), dma((phases, BANDS)), dma((phases,)),
                dma((GROUPS, 4)), dma((GROUPS, 4)), dma((GROUPS, 3)), dma((GROUPS, 3)),
                dma, dma, dma,
            ],
            compiler_params=pltpu.CompilerParams(
                collective_id=phases, has_side_effects=True, vmem_limit_bytes=60 << 20
            ),
            cost_estimate=pl.CostEstimate(flops=2 << 30, bytes_accessed=4 << 20, transcendentals=0),
            name="multiples",
        )(selected, traces, live, jnp.asarray(fwd), jnp.asarray(inv))

    owner = selected // SHOTS
    most = jnp.max(jnp.sum((owner[:, None] == owner[None, :]).astype(I32), axis=1))
    out = lax.cond(most <= SHOTS // 2, lambda: call(2), lambda: call(1))
    return out.transpose(1, 0, 2)[:, None]


def solution(mesh):
    in_specs = (P("af", "row", None), P("af", "row"), P())
    out_specs = P(None, "row", "af", None)
    return jax.shard_map(per_device, mesh=mesh, in_specs=in_specs, out_specs=out_specs, check_vma=False)
```

```python
import functools
import math

import jax
import jax.numpy as jnp
import numpy as np
from jax import lax
from jax.experimental import pallas as pl
from jax.experimental.pallas import tpu as pltpu
from jax.sharding import PartitionSpec as P

MESH = pl.DeviceIdType.MESH
BF, F32, I32 = jnp.bfloat16, jnp.float32, jnp.int32

NX, NY, NZ, NROW = 4, 8, 4, 4
NT, NF, SHOTS, RECV, OUT = 512, 256, 8, 256, 32
BANDS, PER = 32, 8
COMP = 2 * PER
EARLY, CAP = 4, 16
METER = (0, 31, 0)


def host_tables():
    t = np.arange(NT)[:, None]
    f = np.arange(NF)[None, :]
    ang = (t * f % NT) * (2.0 * math.pi / NT)
    norm = 1.0 / math.sqrt(NT)
    w = np.where(np.arange(NF) == 0, 1.0, 2.0)[:, None]
    cos, sin = np.cos(ang).T, -np.sin(ang).T
    fwd = np.stack([cos.reshape(BANDS, PER, NT), sin.reshape(BANDS, PER, NT)], axis=1) * norm
    inv = np.concatenate([cos * w, sin * w], axis=0) * norm
    as_bf = lambda a: a.astype(np.float32).astype(jnp.bfloat16)
    fwd = fwd.reshape(2 * NF, NT)
    return as_bf(np.concatenate([fwd, fwd[:128]])), as_bf(inv)


def af(x, y, z):
    return (x * NY + y) * NZ + z


def base_of(y):
    return lax.rem(y - 2 + lax.rem(y, 2) + NY, NY)


def iota(shape, dim):
    return lax.broadcasted_iota(I32, shape, dim)


def mm(a, b, dims=((1,), (0,))):
    return lax.dot_general(a, b, (dims, ((), ())), preferred_element_type=F32)


def kernel(
    early, cap, sel_hbm, traces_hbm, live_hbm, fwd_hbm, inv_hbm, out_ref,
    sel_ref, src_ref, place_ref, group_ref, live_ref, traces, fwd, inv, send_a, send_b, recv_a, recv_b,
    bt, turn, pack, picked, lanes, expand, spread, a_own, a_msg, a_in, a_row, p2, stage, r_send, r_recv,
    load_sem, send_sem, recv_sem, own_sem, a_send_sem, a_recv_sem, row_send_sem, row_recv_sem,
    r_send_sem, r_recv_sem, r_own_sem, homes_sem,
):
    phases = 1 if early == SHOTS else 2
    sends, recvs = (send_a, send_b), (recv_a, recv_b)
    parts = ((0, early), (early, SHOTS))

    a = lax.axis_index("af")
    row = lax.axis_index("row")
    x, y, z = lax.div(a, NY * NZ), lax.rem(lax.div(a, NZ), NY), lax.rem(a, NZ)
    half, zp, zs, odd = lax.div(y, 2), lax.div(z, 2), lax.rem(z, 2), lax.rem(y, 2)
    base = base_of(y)
    xs = [lax.rem(x + i, NX) for i in range(NX)]
    ys = [lax.rem(y + i, NY) for i in range(NY)]
    zz = [lax.rem(z + i, NZ) for i in range(NZ)]
    other = lax.rem(row + 2, NROW)
    cores = (a, row + 1 - 2 * lax.rem(row, 2))
    pair = [z, z + 1 - 2 * zs]
    to_y = [lax.rem(2 * half - 1 + lax.rem(odd + 1 + w, 4) + NY, NY) for w in range(4)]
    from_y = [lax.rem(base + lax.rem(lax.rem(y - base + NY, NY) + w, 4), NY) for w in range(4)]
    homes = [af(x, ys[4 * (u // 2)], zz[2 * (u % 2)]) for u in range(4)]

    fwd_copy = pltpu.make_async_copy(fwd_hbm, fwd, load_sem.at[SHOTS])
    inv_copy = pltpu.make_async_copy(inv_hbm, inv, load_sem.at[SHOTS + 1])
    live_copy = pltpu.make_async_copy(live_hbm, live_ref, load_sem.at[SHOTS + 2])
    sel_copy = pltpu.make_async_copy(sel_hbm, sel_ref, load_sem.at[SHOTS + 3])
    sel_copy.start()
    fwd_copy.start()
    live_copy.start()
    loads = [pltpu.make_async_copy(traces_hbm.at[s], traces.at[s], load_sem.at[s]) for s in range(SHOTS)]
    for c in loads:
        c.start()
    inv_copy.start()

    barrier = pltpu.get_barrier_semaphore()

    pl.semaphore_signal(barrier, inc=1, device_id=(a, other), device_id_type=MESH)
    for u in range(1, 4):
        pl.semaphore_signal(barrier, inc=1, device_id=(homes[u], row), device_id_type=MESH)
    pl.semaphore_signal(barrier, inc=1, device_id=cores, device_id_type=MESH)
    for i in range(1, BANDS):
        pl.semaphore_signal(
            barrier, inc=1, device_id=(af(xs[i // 8], from_y[i // 2 % 4], pair[i % 2]), row), device_id_type=MESH
        )

    sel_copy.wait()
    chosen = [sel_ref[o] - a * SHOTS for o in range(OUT)]
    flag = [sum((c == s).astype(I32) for c in chosen) for s in range(SHOTS)]
    count = sum(flag)
    place, ahead = [], 0
    for s in range(SHOTS):
        place.append(jnp.where(flag[s] > 0, ahead, count + s - ahead))
        ahead = ahead + flag[s]
    shot_at = [sum(jnp.where(place[s] == n, s, 0) for s in range(SHOTS)) for n in range(SHOTS)]

    fwd_copy.wait()
    live_copy.wait()
    for c in loads:
        c.wait()

    def band_of(bx, hy, hz):
        return bx * 8 + lax.rem(hy, 4) * 2 + lax.rem(hz, 2)

    to_slot = [x * 8 + lax.rem(y - base_of(hy) + NY, NY) * 2 + zs for hy in to_y]

    def band_copy(ph, dx, w, dz):
        band, slot = band_of(xs[dx], to_y[w], pair[dz]), to_slot[w]
        return pltpu.make_async_remote_copy(
            src_ref=sends[ph].at[band], dst_ref=recvs[ph].at[slot],
            send_sem=send_sem.at[(dx * 4 + w) * 2 + dz if ph < phases - 1 else 0],
            recv_sem=recv_sem.at[ph, slot], device_id=(af(xs[dx], to_y[w], pair[dz]), row), device_id_type=MESH,
        )

    own_band, own_slot = band_of(x, y, z), to_slot[0]
    own_copies = [
        pltpu.make_async_copy(sends[ph].at[own_band], recvs[ph].at[own_slot], own_sem.at[ph]) for ph in range(phases)
    ]
    order = [
        [((1 + 2 * i + j % 2) % NX, (j // 2 + 1) % 4, (j // 8 + 1) % 2) for j in range(16)] for i in range(2)
    ]
    order = [[t for t in part if t != (0, 0, 0)] for part in order]

    for ph in range(phases):
        for i in range(2):
            first = xs[(1 + 2 * i) % NX]
            second = xs[(2 + 2 * i) % NX]
            table = fwd[pl.ds(pl.multiple_of(first * 128, 128), 256), :]
            for n in range(*parts[ph]):
                shot = shot_at[n]
                spec = mm(table, traces[shot], ((1,), (1,))) * live_ref[pl.ds(shot, 1), :].astype(F32)
                spec = spec.astype(BF).reshape(2, 8, COMP, RECV)
                sends[ph][pl.ds(first * 8, 8), n - parts[ph][0]] = spec[0]
                sends[ph][pl.ds(second * 8, 8), n - parts[ph][0]] = spec[1]
            if ph == 0:
                if i == 0:
                    pl.semaphore_wait(barrier, BANDS - 1 + 1 + 3 + 1)
                    pl.semaphore_signal(homes_sem, inc=1, device_id=(a, other), device_id_type=MESH)
                for t in order[i]:
                    band_copy(0, *t).start()
        own_copies[ph].start()

    ro, co = iota((256, 256), 0), iota((256, 256), 1)
    n, s = ro % 16 // SHOTS, ro % SHOTS
    from_a, from_b = n * early + s, 2 * early + n * (SHOTS - early) + s - early
    turn[...] = jnp.where(co == jnp.where(s < early, from_a, from_b) * 16 + ro // 16, 1.0, 0.0).astype(BF)
    line = jnp.full((1, 128), -1, I32)
    for o in range(OUT):
        line = jnp.where(iota((1, 128), 1) == o, sel_ref[o], line)

    @pl.loop(0, OUT)
    def _(o):
        shot = sel_ref[o]
        owner = lax.div(shot, SHOTS)
        rank = sum(
            ((lax.div(sel_ref[p], SHOTS) == owner) & (sel_ref[p] < shot)).astype(I32) for p in range(OUT)
        )
        dy = lax.rem(lax.rem(lax.div(owner, NZ), NY) - base + NY, NY)
        oz = lax.rem(owner, NZ)
        src_ref[o] = lax.div(owner, NY * NZ) * 8 + lax.rem(dy, 4) * 2 + lax.rem(oz, 2)
        place_ref[o] = jnp.minimum(rank, early - 1)
        group_ref[o] = lax.div(dy, 4) * 2 + jnp.where(lax.div(oz, 2) == zp, 0, 1)

    per_cap = PER * cap
    to_pack = jnp.full((1, 512), -1, I32)
    to_expand = jnp.full((OUT, 128), 0, I32)
    counts = [0] * 4
    for o in range(OUT):
        group = group_ref[o]
        rank = sum(jnp.where(group == v, counts[v], 0) for v in range(4))
        counts = [counts[v] + (group == v).astype(I32) for v in range(4)]
        to_pack = jnp.where((iota((1, 512), 1) // COMP == o) & (group == 0), rank, to_pack)
        to_expand = jnp.where(iota((OUT, 128), 0) == o, group * per_cap + rank, to_expand)
    pr = iota((COMP * cap, 512), 0)
    pack[...] = jnp.where(
        (iota((COMP * cap, 512), 1) % COMP == pr // cap) & (to_pack == pr % cap), 1.0, 0.0
    ).astype(BF)
    for f in range(PER):
        expand[f * OUT : (f + 1) * OUT, :] = jnp.where(
            iota((OUT, 4 * per_cap), 1) == to_expand[:, 0:1] + f * cap, 1.0, 0.0
        ).astype(BF)

    r_at = iota((256, 128), 0)
    here = jnp.where((row * RECV + r_at == line) & (iota((256, 128), 1) < OUT), 1.0, 0.0)
    same = ro // SHOTS == co // SHOTS
    ahead_of = mm(jnp.where(same & (co < ro), 1.0, 0.0).astype(BF), here.astype(BF))
    all_of = mm(jnp.where(same, 1.0, 0.0).astype(BF), here.astype(BF))
    total_of = lambda v: jnp.sum(v, axis=1, keepdims=True).astype(I32)
    n_here, n_ahead, n_all = total_of(here), total_of(ahead_of), total_of(all_of)
    r1 = iota((256, 1), 0)
    at = jnp.where(n_here > 0, n_ahead, n_all + r1 % SHOTS - n_ahead)
    ry, rz = (r1 // (NZ * SHOTS) - base + NY) % NY, r1 // SHOTS % NZ
    u = ry // 4 * 2 + jnp.where(rz // 2 == zp, 0, 1)
    to = u * 128 + (ry % 4 * 2 + rz % 2) * SHOTS + at
    for p in range(2):
        lanes[p * 256 : (p + 1) * 256, :] = jnp.where(iota((256, 512), 1) == to + p * 64, 1.0, 0.0).astype(BF)
    d_at = iota((128, 512), 0)
    j2 = iota((128, 512), 1)
    spread[...] = jnp.where(j2 % 256 == 2 * d_at + j2 // 256, 1.0, 0.0).astype(BF)
    p2[...] = jnp.zeros_like(p2)

    def second_phase(start, stop):
        for t in (order[0] + order[1])[start:stop] if phases == 2 else ():
            band_copy(0, *t).wait_send()
            band_copy(1, *t).start()

    second_phase(0, METER[0])

    def await_from(ph, sx):
        for q in range(8):
            slot = sx * 8 + q

            @pl.when(slot != own_slot)
            def _():
                pltpu.make_async_remote_copy(
                    src_ref=sends[ph].at[0], dst_ref=recvs[ph].at[slot], send_sem=send_sem.at[0],
                    recv_sem=recv_sem.at[ph, slot], device_id=cores, device_id_type=MESH,
                ).wait_recv()

    def arrive(start, stop):
        @pl.loop(start, stop)
        def _(i):
            sx = lax.rem(x + 2 * NX - 1 - i, NX)
            if phases == 2:
                await_from(1, sx)
            for q in range(4):
                block = [
                    recvs[ph][pl.ds(sx * 8 + q * 2, 2)].reshape(-1, RECV) for ph in range(phases)
                ]
                turned = mm(turn[...], jnp.concatenate(block, axis=0)).astype(BF).reshape(2, PER, 16, RECV)
                bt[:, sx, 0, q] = turned[0]
                bt[:, sx, 1, q] = turned[1]

    for c in own_copies:
        c.wait()

    @pl.loop(0, NX)
    def _(i):
        await_from(0, lax.rem(x + 2 * NX - 1 - i, NX))

    def home_copy(side, v):
        sem = side * 4 + v
        return pltpu.make_async_remote_copy(
            src_ref=a_msg.at[v], dst_ref=a_in.at[side, v], send_sem=a_send_sem.at[sem],
            recv_sem=a_recv_sem.at[sem], device_id=(homes[v], (row, other)[side]), device_id_type=MESH,
        )

    def core_copy(slot, sem):
        return pltpu.make_async_remote_copy(
            src_ref=a_row.at[slot], dst_ref=a_row.at[slot], send_sem=row_send_sem.at[sem],
            recv_sem=row_recv_sem.at[sem], device_id=cores, device_id_type=MESH,
        )

    for o in range(OUT):
        picked[o] = recv_a[src_ref[o], place_ref[o]]
    got = mm(pack[...], picked[...].reshape(OUT * COMP, RECV)).astype(BF).reshape(2, PER, cap, RECV)
    for f in range(PER):
        a_own[f * cap : (f + 1) * cap, 0:RECV] = got[0, f]
        a_own[f * cap : (f + 1) * cap, RECV:] = got[1, f]
    pl.semaphore_wait(homes_sem, 1)
    for v in (3, 2, 1, 0):
        msg = mm(a_own[...], lanes[:, v * 128 : (v + 1) * 128]).astype(BF)
        a_msg[v] = msg
        home_copy(1, v).start()
        if v:
            home_copy(0, v).start()
        else:
            a_in[0, 0] = msg

    second_phase(METER[0], METER[1])

    if phases == 2 and METER[2]:
        arrive(0, METER[2])
    for v in (1, 2, 3):
        home_copy(0, v).wait()
    a_row[row] = mm(expand[...], a_in[0].reshape(4 * per_cap, 128)).astype(BF)
    near = core_copy(row, 0)
    near.start()
    for v in range(4):
        home_copy(1, v).wait()
    a_row[other] = mm(expand[...], a_in[1].reshape(4 * per_cap, 128)).astype(BF)
    far = core_copy(other, 1)
    far.start()
    second_phase(METER[1], BANDS)
    arrive(METER[2] if phases == 2 else 0, NX)
    near.wait_recv()
    far.wait_recv()

    imag = iota((1, 128), 1) >= 64
    sign = jnp.where(imag, -1.0, 1.0)
    factor = 1.0 / math.sqrt(NX * NY * NZ * SHOTS)
    left = []
    for v in range(NROW):
        val = a_row[v].astype(F32)
        left.append(((val * sign).astype(BF), pltpu.roll(val, 64, 1).astype(BF)))
    for f in range(PER):
        rows = slice(f * OUT, (f + 1) * OUT)
        lhs = jnp.concatenate(
            [jnp.concatenate([left[v][p][rows] for v in range(NROW)], axis=1) for p in range(2)], axis=0
        )
        pred = (mm(lhs, bt[f].reshape(512, RECV)) * factor).astype(BF)
        p2[f, 0:64, 0:RECV] = pred
        p2[f, 64:128, RECV:] = pred

    for f in range(PER):
        stage[pl.ds(f, 128, stride=8), :] = mm(spread[...], p2[f], ((1,), (1,)))
    r_send[...] = stage[...].astype(BF).reshape(128, 8, 128)

    my_slot = (lax.div(y, 4) * 2 + zp) * BANDS + own_band
    own_r = pltpu.make_async_copy(r_send.at[a], r_recv.at[my_slot], r_own_sem)
    own_r.start()

    def back(d):
        pltpu.make_async_remote_copy(
            src_ref=r_send.at[d], dst_ref=r_recv.at[my_slot], send_sem=r_send_sem,
            recv_sem=r_recv_sem, device_id=(d, row), device_id_type=MESH,
        ).start()

    @pl.loop(0, NX)
    def _(i):
        dx = lax.rem(x + 2 + i, NX)
        for j in range(31):
            back(af(dx, ys[(4, 3, 5, 2, 6, 1, 7, 0)[j % NY]], zz[(2, 1, 3, 0)[j // NY]]))

        @pl.when(i != 2)
        def _():
            back(af(dx, y, z))

    all_r = pltpu.make_async_remote_copy(
        src_ref=r_send.at[pl.ds(0, 127)], dst_ref=r_recv.at[pl.ds(0, 127)], send_sem=r_send_sem,
        recv_sem=r_recv_sem, device_id=cores, device_id_type=MESH,
    )
    inv_copy.wait()
    own_r.wait()
    all_r.wait_recv()

    total = r_recv[0:32].astype(F32)
    for v in range(1, 4):
        total = total + r_recv[v * 32 : (v + 1) * 32].astype(F32)
    turned = total.reshape(256, 128).T.astype(BF)
    lhs = jnp.concatenate(
        [jnp.concatenate([turned[r * 64 : r * 64 + 32], turned[r * 64 + 32 : r * 64 + 64]], axis=1) for r in range(2)],
        axis=0,
    )
    res = mm(lhs, inv[...])
    for r in range(2):
        out_ref[r] = res[r * 32 : (r + 1) * 32]

    all_r.wait_send()
    near.wait_send()
    far.wait_send()
    pltpu.make_async_remote_copy(
        src_ref=sends[phases - 1].at[pl.ds(0, 31)], dst_ref=recvs[phases - 1].at[pl.ds(0, 31)],
        send_sem=send_sem.at[0], recv_sem=recv_sem.at[0, 0], device_id=cores, device_id_type=MESH,
    ).wait_send()


def per_device(traces, live, selected):
    fwd, inv = host_tables()
    any_, vmem = pl.BlockSpec(memory_space=pl.ANY), pl.BlockSpec(memory_space=pltpu.VMEM)
    dma = pltpu.SemaphoreType.DMA

    def call(early, cap):
        late = max(SHOTS - early, 1)
        return pl.pallas_call(
            functools.partial(kernel, early, cap),
            out_shape=jax.ShapeDtypeStruct((2, OUT, NT), F32),
            in_specs=[any_] * 5,
            out_specs=vmem,
            scratch_shapes=[
                pltpu.SMEM((OUT,), I32),
                pltpu.SMEM((OUT,), I32),
                pltpu.SMEM((OUT,), I32),
                pltpu.SMEM((OUT,), I32),
                pltpu.VMEM((SHOTS, RECV), I32),
                pltpu.VMEM((SHOTS, RECV, NT), BF),
                pltpu.VMEM((2 * NF + 128, NT), BF),
                pltpu.VMEM((2 * NF, NT), BF),
                pltpu.VMEM((BANDS, early, COMP, RECV), BF),
                pltpu.VMEM((BANDS, late, COMP, RECV), BF),
                pltpu.VMEM((BANDS, early, COMP, RECV), BF),
                pltpu.VMEM((BANDS, late, COMP, RECV), BF),
                pltpu.VMEM((PER, NX, 2, 4, 16, RECV), BF),
                pltpu.VMEM((256, 256), BF),
                pltpu.VMEM((COMP * cap, 512), BF),
                pltpu.VMEM((OUT, COMP, RECV), BF),
                pltpu.VMEM((512, 512), BF),
                pltpu.VMEM((PER * OUT, 4 * PER * cap), BF),
                pltpu.VMEM((128, 512), BF),
                pltpu.VMEM((PER * cap, 512), BF),
                pltpu.VMEM((4, PER * cap, 128), BF),
                pltpu.VMEM((2, 4, PER * cap, 128), BF),
                pltpu.VMEM((NROW, PER * OUT, 128), BF),
                pltpu.VMEM((PER, 128, 512), BF),
                pltpu.VMEM((1024, 128), F32),
                pltpu.VMEM((128, 8, 128), BF),
                pltpu.VMEM((128, 8, 128), BF),
                dma((SHOTS + 4,)), dma((BANDS,)), dma((2, BANDS)), dma((2,)),
                dma((8,)), dma((8,)), dma((2,)), dma((2,)),
                dma, dma, dma, pltpu.SemaphoreType.REGULAR,
            ],
            compiler_params=pltpu.CompilerParams(
                collective_id=early, has_side_effects=True, vmem_limit_bytes=60 << 20
            ),
            cost_estimate=pl.CostEstimate(flops=2 << 30, bytes_accessed=4 << 20, transcendentals=0),
            name="multiples",
        )(selected, traces, live, jnp.asarray(fwd), jnp.asarray(inv))

    owner = selected // SHOTS
    zone = owner // NZ % NY // 2 * 2 + owner % NZ // 2
    at = jnp.arange(8, dtype=I32)[:, None]
    member = (zone[None, :] == at) | (zone[None, :] == (at + 2) % 8)
    held = jnp.concatenate([(owner[:, None] == owner[None, :]).astype(I32) * (CAP + 1), member.astype(I32) * (EARLY + 1)])
    fits = jnp.max(jnp.sum(held, axis=1)) < (CAP + 1) * (EARLY + 1)
    out = lax.cond(fits, lambda: call(EARLY, CAP), lambda: call(SHOTS, OUT))
    return out.transpose(1, 0, 2)[:, None]


def solution(mesh):
    in_specs = (P("af", "row", None), P("af", "row"), P())
    out_specs = P(None, "row", "af", None)
    return jax.shard_map(per_device, mesh=mesh, in_specs=in_specs, out_specs=out_specs, check_vma=False)
```

```python
import functools
import math

import jax
import jax.numpy as jnp
import numpy as np
from jax import lax
from jax.experimental import pallas as pl
from jax.experimental.pallas import tpu as pltpu
from jax.sharding import PartitionSpec as P

MESH = pl.DeviceIdType.MESH
BF, F32, I32 = jnp.bfloat16, jnp.float32, jnp.int32

NX, NY, NZ, NROW = 4, 8, 4, 4
NT, NF, SHOTS, RECV, OUT = 512, 256, 8, 256, 32
BANDS, PER = 32, 8
COMP = 2 * PER
EARLY, CAP = 4, 16
METER = (0, 31, 0)


def host_tables():
    t = np.arange(NT)[:, None]
    f = np.arange(NF)[None, :]
    ang = (t * f % NT) * (2.0 * math.pi / NT)
    norm = 1.0 / math.sqrt(NT)
    w = np.where(np.arange(NF) == 0, 1.0, 2.0)[:, None]
    cos, sin = np.cos(ang).T, -np.sin(ang).T
    fwd = np.stack([cos.reshape(BANDS, PER, NT), sin.reshape(BANDS, PER, NT)], axis=1) * norm
    inv = np.concatenate([cos * w, sin * w], axis=0) * norm
    as_bf = lambda a: a.astype(np.float32).astype(jnp.bfloat16)
    fwd = fwd.reshape(2 * NF, NT)
    return as_bf(np.concatenate([fwd, fwd[:128]])), as_bf(inv)


def af(x, y, z):
    return (x * NY + y) * NZ + z


def base_of(y):
    return lax.rem(y - 2 + lax.rem(y, 2) + NY, NY)


def iota(shape, dim):
    return lax.broadcasted_iota(I32, shape, dim)


def mm(a, b, dims=((1,), (0,))):
    return lax.dot_general(a, b, (dims, ((), ())), preferred_element_type=F32)


def kernel(
    early, cap, sel_hbm, traces_hbm, live_hbm, fwd_hbm, inv_hbm, out_ref,
    sel_ref, src_ref, place_ref, group_ref, live_ref, traces, fwd, inv, send_a, send_b, recv_a, recv_b,
    bt, turn, pack, picked, lanes, expand, spread, a_own, a_msg, a_in, a_row, p2, stage, r_send, r_recv,
    load_sem, send_sem, recv_sem, own_sem, a_send_sem, a_recv_sem, row_send_sem, row_recv_sem,
    r_send_sem, r_recv_sem, r_own_sem, homes_sem,
):
    phases = 1 if early == SHOTS else 2
    sends, recvs = (send_a, send_b), (recv_a, recv_b)
    parts = ((0, early), (early, SHOTS))

    a = lax.axis_index("af")
    row = lax.axis_index("row")
    x, y, z = lax.div(a, NY * NZ), lax.rem(lax.div(a, NZ), NY), lax.rem(a, NZ)
    half, zp, zs, odd = lax.div(y, 2), lax.div(z, 2), lax.rem(z, 2), lax.rem(y, 2)
    base = base_of(y)
    xs = [lax.rem(x + i, NX) for i in range(NX)]
    ys = [lax.rem(y + i, NY) for i in range(NY)]
    zz = [lax.rem(z + i, NZ) for i in range(NZ)]
    other = lax.rem(row + 2, NROW)
    cores = (a, row + 1 - 2 * lax.rem(row, 2))
    pair = [z, z + 1 - 2 * zs]
    to_y = [lax.rem(2 * half - 1 + lax.rem(odd + 1 + w, 4) + NY, NY) for w in range(4)]
    from_y = [lax.rem(base + lax.rem(lax.rem(y - base + NY, NY) + w, 4), NY) for w in range(4)]
    homes = [af(x, ys[4 * (u // 2)], zz[2 * (u % 2)]) for u in range(4)]

    fwd_copy = pltpu.make_async_copy(fwd_hbm, fwd, load_sem.at[SHOTS])
    inv_copy = pltpu.make_async_copy(inv_hbm, inv, load_sem.at[SHOTS + 1])
    live_copy = pltpu.make_async_copy(live_hbm, live_ref, load_sem.at[SHOTS + 2])
    sel_copy = pltpu.make_async_copy(sel_hbm, sel_ref, load_sem.at[SHOTS + 3])
    sel_copy.start()
    fwd_copy.start()
    live_copy.start()
    loads = [pltpu.make_async_copy(traces_hbm.at[s], traces.at[s], load_sem.at[s]) for s in range(SHOTS)]
    for c in loads:
        c.start()
    inv_copy.start()

    barrier = pltpu.get_barrier_semaphore()

    pl.semaphore_signal(barrier, inc=1, device_id=(a, other), device_id_type=MESH)
    for u in range(1, 4):
        pl.semaphore_signal(barrier, inc=1, device_id=(homes[u], row), device_id_type=MESH)
    pl.semaphore_signal(barrier, inc=1, device_id=cores, device_id_type=MESH)
    for i in range(1, BANDS):
        pl.semaphore_signal(
            barrier, inc=1, device_id=(af(xs[i // 8], from_y[i // 2 % 4], pair[i % 2]), row), device_id_type=MESH
        )

    sel_copy.wait()
    chosen = [sel_ref[o] - a * SHOTS for o in range(OUT)]
    flag = [sum((c == s).astype(I32) for c in chosen) for s in range(SHOTS)]
    count = sum(flag)
    place, ahead = [], 0
    for s in range(SHOTS):
        place.append(jnp.where(flag[s] > 0, ahead, count + s - ahead))
        ahead = ahead + flag[s]
    shot_at = [sum(jnp.where(place[s] == n, s, 0) for s in range(SHOTS)) for n in range(SHOTS)]

    fwd_copy.wait()
    live_copy.wait()
    for c in loads:
        c.wait()

    def band_of(bx, hy, hz):
        return bx * 8 + lax.rem(hy, 4) * 2 + lax.rem(hz, 2)

    to_slot = [x * 8 + lax.rem(y - base_of(hy) + NY, NY) * 2 + zs for hy in to_y]

    def band_copy(ph, dx, w, dz):
        band, slot = band_of(xs[dx], to_y[w], pair[dz]), to_slot[w]
        return pltpu.make_async_remote_copy(
            src_ref=sends[ph].at[band], dst_ref=recvs[ph].at[slot],
            send_sem=send_sem.at[(dx * 4 + w) * 2 + dz if ph < phases - 1 else 0],
            recv_sem=recv_sem.at[ph, slot], device_id=(af(xs[dx], to_y[w], pair[dz]), row), device_id_type=MESH,
        )

    own_band, own_slot = band_of(x, y, z), to_slot[0]
    own_copies = [
        pltpu.make_async_copy(sends[ph].at[own_band], recvs[ph].at[own_slot], own_sem.at[ph]) for ph in range(phases)
    ]
    order = [
        [((1 + 2 * i + j % 2) % NX, (j // 2 + 1) % 4, (j // 8 + 1) % 2) for j in range(16)] for i in range(2)
    ]
    hops = lambda t: min(t[0], NX - t[0]) + (0, 1, 2, 1)[t[1]] + t[2]
    order = [sorted([t for t in part if t != (0, 0, 0)], key=hops, reverse=True) for part in order]

    for ph in range(phases):
        for i in range(2):
            first = xs[(1 + 2 * i) % NX]
            second = xs[(2 + 2 * i) % NX]
            table = fwd[pl.ds(pl.multiple_of(first * 128, 128), 256), :]
            for n in range(*parts[ph]):
                shot = shot_at[n]
                spec = mm(table, traces[shot], ((1,), (1,))) * live_ref[pl.ds(shot, 1), :].astype(F32)
                spec = spec.astype(BF).reshape(2, 8, COMP, RECV)
                sends[ph][pl.ds(first * 8, 8), n - parts[ph][0]] = spec[0]
                sends[ph][pl.ds(second * 8, 8), n - parts[ph][0]] = spec[1]
            if ph == 0:
                if i == 0:
                    pl.semaphore_wait(barrier, BANDS - 1 + 1 + 3 + 1)
                    pl.semaphore_signal(homes_sem, inc=1, device_id=(a, other), device_id_type=MESH)
                for t in order[i]:
                    band_copy(0, *t).start()
        own_copies[ph].start()

    ro, co = iota((256, 256), 0), iota((256, 256), 1)
    n, s = ro % 16 // SHOTS, ro % SHOTS
    from_a, from_b = n * early + s, 2 * early + n * (SHOTS - early) + s - early
    turn[...] = jnp.where(co == jnp.where(s < early, from_a, from_b) * 16 + ro // 16, 1.0, 0.0).astype(BF)
    line = jnp.full((1, 128), -1, I32)
    for o in range(OUT):
        line = jnp.where(iota((1, 128), 1) == o, sel_ref[o], line)

    @pl.loop(0, OUT)
    def _(o):
        shot = sel_ref[o]
        owner = lax.div(shot, SHOTS)
        rank = sum(
            ((lax.div(sel_ref[p], SHOTS) == owner) & (sel_ref[p] < shot)).astype(I32) for p in range(OUT)
        )
        dy = lax.rem(lax.rem(lax.div(owner, NZ), NY) - base + NY, NY)
        oz = lax.rem(owner, NZ)
        src_ref[o] = lax.div(owner, NY * NZ) * 8 + lax.rem(dy, 4) * 2 + lax.rem(oz, 2)
        place_ref[o] = jnp.minimum(rank, early - 1)
        group_ref[o] = lax.div(dy, 4) * 2 + jnp.where(lax.div(oz, 2) == zp, 0, 1)

    per_cap = PER * cap
    to_pack = jnp.full((1, 512), -1, I32)
    to_expand = jnp.full((OUT, 128), 0, I32)
    counts = [0] * 4
    for o in range(OUT):
        group = group_ref[o]
        rank = sum(jnp.where(group == v, counts[v], 0) for v in range(4))
        counts = [counts[v] + (group == v).astype(I32) for v in range(4)]
        to_pack = jnp.where((iota((1, 512), 1) // COMP == o) & (group == 0), rank, to_pack)
        to_expand = jnp.where(iota((OUT, 128), 0) == o, group * per_cap + rank, to_expand)
    pr = iota((COMP * cap, 512), 0)
    pack[...] = jnp.where(
        (iota((COMP * cap, 512), 1) % COMP == pr // cap) & (to_pack == pr % cap), 1.0, 0.0
    ).astype(BF)
    for f in range(PER):
        expand[f * OUT : (f + 1) * OUT, :] = jnp.where(
            iota((OUT, 4 * per_cap), 1) == to_expand[:, 0:1] + f * cap, 1.0, 0.0
        ).astype(BF)

    r_at = iota((256, 128), 0)
    here = jnp.where((row * RECV + r_at == line) & (iota((256, 128), 1) < OUT), 1.0, 0.0)
    same = ro // SHOTS == co // SHOTS
    ahead_of = mm(jnp.where(same & (co < ro), 1.0, 0.0).astype(BF), here.astype(BF))
    all_of = mm(jnp.where(same, 1.0, 0.0).astype(BF), here.astype(BF))
    total_of = lambda v: jnp.sum(v, axis=1, keepdims=True).astype(I32)
    n_here, n_ahead, n_all = total_of(here), total_of(ahead_of), total_of(all_of)
    r1 = iota((256, 1), 0)
    at = jnp.where(n_here > 0, n_ahead, n_all + r1 % SHOTS - n_ahead)
    ry, rz = (r1 // (NZ * SHOTS) - base + NY) % NY, r1 // SHOTS % NZ
    u = ry // 4 * 2 + jnp.where(rz // 2 == zp, 0, 1)
    to = u * 128 + (ry % 4 * 2 + rz % 2) * SHOTS + at
    for p in range(2):
        lanes[p * 256 : (p + 1) * 256, :] = jnp.where(iota((256, 512), 1) == to + p * 64, 1.0, 0.0).astype(BF)
    d_at = iota((128, 512), 0)
    j2 = iota((128, 512), 1)
    spread[...] = jnp.where(j2 % 256 == 2 * d_at + j2 // 256, 1.0, 0.0).astype(BF)
    p2[...] = jnp.zeros_like(p2)

    def second_phase(start, stop):
        for t in (order[0] + order[1])[start:stop] if phases == 2 else ():
            band_copy(0, *t).wait_send()
            band_copy(1, *t).start()

    second_phase(0, METER[0])

    def await_from(ph, sx):
        for q in range(8):
            slot = sx * 8 + q

            @pl.when(slot != own_slot)
            def _():
                pltpu.make_async_remote_copy(
                    src_ref=sends[ph].at[0], dst_ref=recvs[ph].at[slot], send_sem=send_sem.at[0],
                    recv_sem=recv_sem.at[ph, slot], device_id=cores, device_id_type=MESH,
                ).wait_recv()

    def arrive(start, stop):
        @pl.loop(start, stop)
        def _(i):
            sx = lax.rem(x + 2 * NX - 1 - i, NX)
            if phases == 2:
                await_from(1, sx)
            for q in range(4):
                block = [
                    recvs[ph][pl.ds(sx * 8 + q * 2, 2)].reshape(-1, RECV) for ph in range(phases)
                ]
                turned = mm(turn[...], jnp.concatenate(block, axis=0)).astype(BF).reshape(2, PER, 16, RECV)
                bt[:, sx, 0, q] = turned[0]
                bt[:, sx, 1, q] = turned[1]

    for c in own_copies:
        c.wait()

    @pl.loop(0, NX)
    def _(i):
        await_from(0, lax.rem(x + 2 * NX - 1 - i, NX))

    def home_copy(side, v):
        sem = side * 4 + v
        return pltpu.make_async_remote_copy(
            src_ref=a_msg.at[v], dst_ref=a_in.at[side, v], send_sem=a_send_sem.at[sem],
            recv_sem=a_recv_sem.at[sem], device_id=(homes[v], (row, other)[side]), device_id_type=MESH,
        )

    def core_copy(slot, sem):
        return pltpu.make_async_remote_copy(
            src_ref=a_row.at[slot], dst_ref=a_row.at[slot], send_sem=row_send_sem.at[sem],
            recv_sem=row_recv_sem.at[sem], device_id=cores, device_id_type=MESH,
        )

    for o in range(OUT):
        picked[o] = recv_a[src_ref[o], place_ref[o]]
    got = mm(pack[...], picked[...].reshape(OUT * COMP, RECV)).astype(BF).reshape(2, PER, cap, RECV)
    for f in range(PER):
        a_own[f * cap : (f + 1) * cap, 0:RECV] = got[0, f]
        a_own[f * cap : (f + 1) * cap, RECV:] = got[1, f]
    pl.semaphore_wait(homes_sem, 1)
    for v in (3, 2, 1, 0):
        msg = mm(a_own[...], lanes[:, v * 128 : (v + 1) * 128]).astype(BF)
        a_msg[v] = msg
        home_copy(1, v).start()
        if v:
            home_copy(0, v).start()
        else:
            a_in[0, 0] = msg

    second_phase(METER[0], METER[1])

    if phases == 2 and METER[2]:
        arrive(0, METER[2])
    for v in (1, 2, 3):
        home_copy(0, v).wait()
    a_row[row] = mm(expand[...], a_in[0].reshape(4 * per_cap, 128)).astype(BF)
    near = core_copy(row, 0)
    near.start()
    for v in range(4):
        home_copy(1, v).wait()
    a_row[other] = mm(expand[...], a_in[1].reshape(4 * per_cap, 128)).astype(BF)
    far = core_copy(other, 1)
    far.start()
    second_phase(METER[1], BANDS)
    arrive(METER[2] if phases == 2 else 0, NX)
    near.wait_recv()
    far.wait_recv()

    imag = iota((1, 128), 1) >= 64
    sign = jnp.where(imag, -1.0, 1.0)
    factor = 1.0 / math.sqrt(NX * NY * NZ * SHOTS)
    left = []
    for v in range(NROW):
        val = a_row[v].astype(F32)
        left.append(((val * sign).astype(BF), pltpu.roll(val, 64, 1).astype(BF)))
    for f in range(PER):
        rows = slice(f * OUT, (f + 1) * OUT)
        lhs = jnp.concatenate(
            [jnp.concatenate([left[v][p][rows] for v in range(NROW)], axis=1) for p in range(2)], axis=0
        )
        pred = (mm(lhs, bt[f].reshape(512, RECV)) * factor).astype(BF)
        p2[f, 0:64, 0:RECV] = pred
        p2[f, 64:128, RECV:] = pred

    for f in range(PER):
        stage[pl.ds(f, 128, stride=8), :] = mm(spread[...], p2[f], ((1,), (1,)))
    r_send[...] = stage[...].astype(BF).reshape(128, 8, 128)

    my_slot = (lax.div(y, 4) * 2 + zp) * BANDS + own_band
    own_r = pltpu.make_async_copy(r_send.at[a], r_recv.at[my_slot], r_own_sem)
    own_r.start()

    def back(d):
        pltpu.make_async_remote_copy(
            src_ref=r_send.at[d], dst_ref=r_recv.at[my_slot], send_sem=r_send_sem,
            recv_sem=r_recv_sem, device_id=(d, row), device_id_type=MESH,
        ).start()

    @pl.loop(0, NX)
    def _(i):
        dx = lax.rem(x + 2 + i, NX)
        for j in range(31):
            back(af(dx, ys[(4, 3, 5, 2, 6, 1, 7, 0)[j % NY]], zz[(2, 1, 3, 0)[j // NY]]))

        @pl.when(i != 2)
        def _():
            back(af(dx, y, z))

    all_r = pltpu.make_async_remote_copy(
        src_ref=r_send.at[pl.ds(0, 127)], dst_ref=r_recv.at[pl.ds(0, 127)], send_sem=r_send_sem,
        recv_sem=r_recv_sem, device_id=cores, device_id_type=MESH,
    )
    inv_copy.wait()
    own_r.wait()
    all_r.wait_recv()

    total = r_recv[0:32].astype(F32)
    for v in range(1, 4):
        total = total + r_recv[v * 32 : (v + 1) * 32].astype(F32)
    turned = total.reshape(256, 128).T.astype(BF)
    lhs = jnp.concatenate(
        [jnp.concatenate([turned[r * 64 : r * 64 + 32], turned[r * 64 + 32 : r * 64 + 64]], axis=1) for r in range(2)],
        axis=0,
    )
    res = mm(lhs, inv[...])
    for r in range(2):
        out_ref[:, 0, r, :] = res[r * 32 : (r + 1) * 32]

    all_r.wait_send()
    near.wait_send()
    far.wait_send()
    pltpu.make_async_remote_copy(
        src_ref=sends[phases - 1].at[pl.ds(0, 31)], dst_ref=recvs[phases - 1].at[pl.ds(0, 31)],
        send_sem=send_sem.at[0], recv_sem=recv_sem.at[0, 0], device_id=cores, device_id_type=MESH,
    ).wait_send()


def per_device(traces, live, selected):
    fwd, inv = host_tables()
    any_, vmem = pl.BlockSpec(memory_space=pl.ANY), pl.BlockSpec(memory_space=pltpu.VMEM)
    dma = pltpu.SemaphoreType.DMA

    def call(early, cap):
        late = max(SHOTS - early, 1)
        return pl.pallas_call(
            functools.partial(kernel, early, cap),
            out_shape=jax.ShapeDtypeStruct((OUT, 1, 2, NT), F32),
            in_specs=[any_] * 5,
            out_specs=vmem,
            scratch_shapes=[
                pltpu.SMEM((OUT,), I32),
                pltpu.SMEM((OUT,), I32),
                pltpu.SMEM((OUT,), I32),
                pltpu.SMEM((OUT,), I32),
                pltpu.VMEM((SHOTS, RECV), I32),
                pltpu.VMEM((SHOTS, RECV, NT), BF),
                pltpu.VMEM((2 * NF + 128, NT), BF),
                pltpu.VMEM((2 * NF, NT), BF),
                pltpu.VMEM((BANDS, early, COMP, RECV), BF),
                pltpu.VMEM((BANDS, late, COMP, RECV), BF),
                pltpu.VMEM((BANDS, early, COMP, RECV), BF),
                pltpu.VMEM((BANDS, late, COMP, RECV), BF),
                pltpu.VMEM((PER, NX, 2, 4, 16, RECV), BF),
                pltpu.VMEM((256, 256), BF),
                pltpu.VMEM((COMP * cap, 512), BF),
                pltpu.VMEM((OUT, COMP, RECV), BF),
                pltpu.VMEM((512, 512), BF),
                pltpu.VMEM((PER * OUT, 4 * PER * cap), BF),
                pltpu.VMEM((128, 512), BF),
                pltpu.VMEM((PER * cap, 512), BF),
                pltpu.VMEM((4, PER * cap, 128), BF),
                pltpu.VMEM((2, 4, PER * cap, 128), BF),
                pltpu.VMEM((NROW, PER * OUT, 128), BF),
                pltpu.VMEM((PER, 128, 512), BF),
                pltpu.VMEM((1024, 128), F32),
                pltpu.VMEM((128, 8, 128), BF),
                pltpu.VMEM((128, 8, 128), BF),
                dma((SHOTS + 4,)), dma((BANDS,)), dma((2, BANDS)), dma((2,)),
                dma((8,)), dma((8,)), dma((2,)), dma((2,)),
                dma, dma, dma, pltpu.SemaphoreType.REGULAR,
            ],
            compiler_params=pltpu.CompilerParams(
                collective_id=early, has_side_effects=True, vmem_limit_bytes=60 << 20
            ),
            cost_estimate=pl.CostEstimate(flops=2 << 30, bytes_accessed=4 << 20, transcendentals=0),
            name="multiples",
        )(selected, traces, live, jnp.asarray(fwd), jnp.asarray(inv))

    owner = selected // SHOTS
    zone = owner // NZ % NY // 2 * 2 + owner % NZ // 2
    at = jnp.arange(8, dtype=I32)[:, None]
    member = (zone[None, :] == at) | (zone[None, :] == (at + 2) % 8)
    held = jnp.concatenate([(owner[:, None] == owner[None, :]).astype(I32) * (CAP + 1), member.astype(I32) * (EARLY + 1)])
    fits = jnp.max(jnp.sum(held, axis=1)) < (CAP + 1) * (EARLY + 1)
    out = lax.cond(fits, lambda: call(EARLY, CAP), lambda: call(SHOTS, OUT))
    return out


def solution(mesh):
    in_specs = (P("af", "row", None), P("af", "row"), P())
    out_specs = P(None, "row", "af", None)
    return jax.shard_map(per_device, mesh=mesh, in_specs=in_specs, out_specs=out_specs, check_vma=False)
```
